32 devices in a mesh: row: 4 (over y, core), col: 8 (over z, x).
Axes of the slice: x: 2, y: 2, z: 4, core: 2. Of those that a mesh axis runs over, the one named last changes fastest.
Arguments:
- pair_features: bfloat16 [64, 512, 512], P(None, 'col', 'row'), may hold values from -6 to 6
- first_block_kernel: bfloat16 [3, 3, 64, 64], replicated, may hold values from -0.25 to 0.25
- first_block_bias: float32 [64], replicated, may hold values from -3 to 3
- second_block_kernel: bfloat16 [3, 3, 64, 64], replicated, may hold values from -0.25 to 0.25
- second_block_bias: float32 [64], replicated, may hold values from -3 to 3
- head_weight: bfloat16 [37, 64], replicated, may hold values from -32 to 32
- head_bias: float32 [37], replicated, may hold values from -4 to 4
- target: int32 [512, 512], P('col', 'row'), may hold values from 0 to 36
Outputs:
- feat_grad: float32 [64, 512, 512], P(None, 'col', 'row')
The draws below stay inside these ranges and needn't reach their ends.
All inputs are finite; a program needn't handle non-finite values.
Results may differ from the reference program's by a relative error of at most 0.0055.
The reference program's roundings to bfloat16 on the way count: a program that leaves them out, or rounds other values in their place, can miss the bound.
Values may be sent and summed in bfloat16 or wider, within the bound.
No kernel may reach another device: no remote copies, remote signals or barrier semaphores. Data moves between devices by JAX's collectives and lax.ppermute only.
A program may use at most 64 MiB of HBM per device.

```python
import math
import jax
import jax.numpy as jnp
from jax import lax

C = 64
NB = 37
DILATION_FIRST = 4
DILATION_SECOND = 8
RESIDUES = 512


def draw_head_weight(key, part):
    key_main = jax.random.fold_in(key, 0)
    gaussian = jax.random.normal(key_main, (NB, C), jnp.float32)
    scaled = 3.0 / math.sqrt(C) * gaussian
    return jnp.clip(scaled, -32.0, 32.0).astype(jnp.bfloat16)


def set_ends(entries, rng, least, largest):
    index_at = [jax.random.randint(jax.random.fold_in(rng, axis), (), 0, length) for axis, length in enumerate(entries.shape)]
    main_axis = entries.shape.index(max(entries.shape))
    next_to = index_at[:main_axis] + [(index_at[main_axis] + 1) % entries.shape[main_axis]] + index_at[main_axis + 1:]
    return entries.at[tuple(index_at)].set(least).at[tuple(next_to)].set(largest)


def levels(own_key, dims, pieces, low, top_value):
    level = 1.0
    for dim, parts in pieces:
        draws = jax.random.uniform(jax.random.fold_in(jax.random.fold_in(own_key, 6), dim), (parts,), jnp.float32, low / len(pieces), top_value / len(pieces))
        level = level * jnp.repeat(jnp.exp(draws), dims[dim] // parts).reshape((-1,) + (1,) * (len(dims) - 1 - dim))
    return level


def noise(own_key, shape, deviation, limit, shards=(), kind=jnp.bfloat16):
    values = deviation * jax.random.normal(own_key, shape, jnp.float32)
    if shards:
        values = values * levels(own_key, shape, shards, -0.22, 0.18)
    return jnp.clip(values, -limit, limit).astype(kind)


def setup_inputs(seed: int = 0) -> dict:
    splits = jax.random.split(jax.random.key(seed), 9)
    return {
        "pair_features": noise(splits[0], (C, RESIDUES, RESIDUES), 1.0, 6.0, ((1, 8), (2, 4))),
        "first_block_kernel": noise(splits[1], (3, 3, C, C), (9 * C) ** -0.5, 0.25),
        "first_block_bias": noise(splits[2], (C,), 0.5, 3.0, (), jnp.float32),
        "second_block_kernel": noise(splits[3], (3, 3, C, C), (9 * C) ** -0.5, 0.25),
        "second_block_bias": noise(splits[4], (C,), 0.5, 3.0, (), jnp.float32),
        "head_weight": draw_head_weight(jax.random.fold_in(splits[8], 71), 0),
        "head_bias": noise(splits[6], (NB,), 1.0, 4.0, (), jnp.float32),
        "target": set_ends(jax.random.randint(splits[7], (RESIDUES, RESIDUES), 0, NB), jax.random.fold_in(splits[7], 1), 0, NB - 1).astype(jnp.int32),
    }


def rounded(tensor):
    return lax.optimization_barrier(tensor.astype(jnp.bfloat16))


def activate(pre_act):
    return jnp.where(pre_act > 0, pre_act, jnp.exp(jnp.minimum(pre_act, 0.0)) - 1.0)


def slope(pre_act):
    return jnp.where(pre_act > 0, 1.0, jnp.exp(jnp.minimum(pre_act, 0.0)))


def flipped_kernel(kernel):
    return jnp.transpose(kernel[::-1, ::-1], (0, 1, 3, 2))


def dilated_kernel(source, kernel, spacing):
    channels, first_len, second_len = source.shape
    padded_input = jnp.pad(source, ((0, 0), (spacing, spacing), (spacing, spacing)))
    summed = jnp.zeros((kernel.shape[2], first_len * second_len), jnp.float32)
    for tap_first in range(3):
        for tap_second in range(3):
            window = padded_input[:, tap_first * spacing:tap_first * spacing + first_len, tap_second * spacing:tap_second * spacing + second_len]
            summed = summed + jnp.dot(kernel[tap_first, tap_second], window.reshape(channels, -1), preferred_element_type=jnp.float32)
    return summed.reshape(kernel.shape[2], first_len, second_len)


def reference(pair_features, first_block_kernel, first_block_bias, second_block_kernel, second_block_bias, head_weight, head_bias, target):
    channels, first_len, second_len = pair_features.shape
    first_preactivation = pair_features.astype(jnp.float32) + dilated_kernel(pair_features, first_block_kernel, DILATION_FIRST) + first_block_bias[:, None, None]
    first_hidden = rounded(activate(first_preactivation))
    second_preactivation = first_hidden.astype(jnp.float32) + dilated_kernel(first_hidden, second_block_kernel, DILATION_SECOND) + second_block_bias[:, None, None]
    hidden_two = rounded(activate(second_preactivation))
    mirrored = jnp.swapaxes(hidden_two, 1, 2)
    symmetric = rounded(hidden_two.astype(jnp.float32) + mirrored.astype(jnp.float32))
    logits = jnp.dot(head_weight, symmetric.reshape(channels, -1), preferred_element_type=jnp.float32) + head_bias[:, None]
    probability = jax.nn.softmax(logits, axis=0)
    labels = (jnp.arange(NB, dtype=jnp.int32)[:, None] == target.reshape(1, -1)).astype(jnp.float32)
    grad_bins = rounded(probability - labels).reshape(NB, first_len, second_len)
    bins_sum = rounded(grad_bins.astype(jnp.float32) + jnp.swapaxes(grad_bins, 1, 2).astype(jnp.float32))
    grad_two = jnp.dot(head_weight.T, bins_sum.reshape(NB, -1), preferred_element_type=jnp.float32).reshape(channels, first_len, second_len)
    second_delta = rounded(grad_two * slope(second_preactivation))
    first_gradient = second_delta.astype(jnp.float32) + dilated_kernel(second_delta, flipped_kernel(second_block_kernel), DILATION_SECOND)
    first_delta = rounded(first_gradient * slope(first_preactivation))
    return first_delta.astype(jnp.float32) + dilated_kernel(first_delta, flipped_kernel(first_block_kernel), DILATION_FIRST)
```

```python
import jax
import jax.numpy as jnp
from jax import lax
from jax.sharding import PartitionSpec as P

DILATION_FIRST = 4
DILATION_SECOND = 8


def padded(cells, sides, width):
    for axis, dim in sides:
        count = lax.axis_size(axis)
        ends = count - 1
        head = lax.slice_in_dim(cells, 0, width, axis=dim)
        tail = lax.slice_in_dim(cells, cells.shape[dim] - width, cells.shape[dim], axis=dim)
        cells = jnp.concatenate(
            [
                lax.ppermute(tail, axis, [(i, (i + 1) % count) for i in range(ends)]),
                cells,
                lax.ppermute(head, axis, [((i + 1) % count, i) for i in range(ends)]),
            ],
            axis=dim,
        )
    return cells


def rounded(tensor):
    return lax.optimization_barrier(tensor.astype(jnp.bfloat16))


def activate(pre_act):
    return jnp.where(pre_act > 0, pre_act, jnp.exp(jnp.minimum(pre_act, 0.0)) - 1.0)


def slope(pre_act):
    return jnp.where(pre_act > 0, 1.0, jnp.exp(jnp.minimum(pre_act, 0.0)))


def flipped_kernel(kernel):
    return jnp.transpose(kernel[::-1, ::-1], (0, 1, 3, 2))


def conv(source, kernel, spacing):
    return lax.conv_general_dilated(
        source[None],
        kernel,
        (1, 1),
        "VALID",
        rhs_dilation=(spacing, spacing),
        dimension_numbers=("NCHW", "HWOI", "NCHW"),
        preferred_element_type=jnp.float32,
    )[0]


def inside_map(shape, margin, tile):
    first = lax.axis_index("col") * tile[0] - margin + jnp.arange(shape[0])
    second = lax.axis_index("row") * tile[1] - margin + jnp.arange(shape[1])
    ok_first = (first >= 0) & (first < tile[0] * lax.axis_size("col"))
    ok_second = (second >= 0) & (second < tile[1] * lax.axis_size("row"))
    return (ok_first[:, None] & ok_second[None, :])[None]


def mirror(tile_block):
    col_count, row_count = lax.axis_size("col"), lax.axis_size("row")
    group = col_count // row_count
    size = tile_block.shape[1]
    mine = lax.axis_index("col") % group
    received = []
    for step in range(group):
        piece = lax.dynamic_slice_in_dim(
            tile_block, ((mine + step) % group) * size, size, axis=2
        )
        pairs = [
            (
                r * col_count + c,
                (c // group) * col_count + group * r + (c % group + step) % group,
            )
            for c in range(col_count)
            for r in range(row_count)
        ]
        received.append(lax.ppermute(piece, ("row", "col"), pairs))
    stacked = jnp.stack((received[::-1] * 2)[:-1])
    ordered = lax.dynamic_slice_in_dim(stacked, group - 1 - mine, group, axis=0)
    return ordered.transpose(1, 3, 0, 2).reshape(tile_block.shape)


def local(
    pair_features,
    first_block_kernel,
    first_block_bias,
    second_block_kernel,
    second_block_bias,
    head_weight,
    head_bias,
    target,
):
    channels, column_count, row_count = pair_features.shape
    tile = (column_count, row_count)
    bins_count = head_weight.shape[0]
    margin = DILATION_FIRST + DILATION_SECOND
    sides = (("row", 2), ("col", 1))
    target_mirror = mirror(target[None])[0]
    wide_input = padded(pair_features, sides, margin)
    d1, d2 = DILATION_FIRST, DILATION_SECOND
    wide_pre_one = (
        wide_input[:, d1:-d1, d1:-d1].astype(jnp.float32)
        + conv(wide_input, first_block_kernel, d1)
        + first_block_bias[:, None, None]
    )
    inside = inside_map(wide_pre_one.shape[1:], d2, tile)
    wide_hidden = rounded(jnp.where(inside, activate(wide_pre_one), 0.0))
    pre_two = (
        wide_hidden[:, d2:-d2, d2:-d2].astype(jnp.float32)
        + conv(wide_hidden, second_block_kernel, d2)
        + second_block_bias[:, None, None]
    )
    hidden_two = rounded(activate(pre_two))
    mirrored = mirror(hidden_two)
    symmetric = rounded(hidden_two.astype(jnp.float32) + mirrored.astype(jnp.float32))
    logits = (
        jnp.dot(head_weight, symmetric.reshape(channels, -1), preferred_element_type=jnp.float32)
        + head_bias[:, None]
    )
    probability = jax.nn.softmax(logits, axis=0)
    bin_ids = jnp.arange(bins_count, dtype=jnp.int32)[:, None]
    grad_bins = rounded(probability - (bin_ids == target.reshape(1, -1)).astype(jnp.float32))
    grad_mirror = rounded(
        probability - (bin_ids == target_mirror.reshape(1, -1)).astype(jnp.float32)
    )
    bins_sum = rounded(grad_bins.astype(jnp.float32) + grad_mirror.astype(jnp.float32))
    grad_two = jnp.dot(head_weight.T, bins_sum, preferred_element_type=jnp.float32).reshape(
        channels, column_count, row_count
    )
    delta_two = rounded(grad_two * slope(pre_two))
    wide_delta_two = padded(delta_two, sides, margin)
    wide_grad_one = wide_delta_two[:, d2:-d2, d2:-d2].astype(jnp.float32) + conv(
        wide_delta_two, flipped_kernel(second_block_kernel), d2
    )
    crop = d2 - d1
    near_pre_one = wide_pre_one[:, crop:-crop, crop:-crop]
    near_inside = inside[:, crop:-crop, crop:-crop]
    delta_one = rounded(jnp.where(near_inside, wide_grad_one * slope(near_pre_one), 0.0))
    return delta_one[:, d1:-d1, d1:-d1].astype(jnp.float32) + conv(
        delta_one, flipped_kernel(first_block_kernel), d1
    )


def solution(mesh):
    in_specs = (P(None, "col", "row"), P(), P(), P(), P(), P(), P(), P("col", "row"))
    out_specs = P(None, "col", "row")
    return jax.shard_map(local, mesh=mesh, in_specs=in_specs, out_specs=out_specs, check_vma=False)
```

```python
import functools

import jax
import jax.numpy as jnp
from jax import lax
from jax.experimental import pallas as pl
from jax.experimental.pallas import tpu as pltpu
from jax.sharding import PartitionSpec as P

DILATION_FIRST = 4
DILATION_SECOND = 8
MARGIN = DILATION_FIRST + DILATION_SECOND
SLOT = 16
F32 = jnp.float32
BF16 = jnp.bfloat16
VMEM = pl.BlockSpec(memory_space=pltpu.VMEM)
SMEM = pl.BlockSpec(memory_space=pltpu.SMEM)


def params(megabytes):
    return pltpu.CompilerParams(vmem_limit_bytes=megabytes << 20)


def lanes_of(shape):
    return lax.broadcasted_iota(jnp.int32, shape, len(shape) - 1)


def pack_edges(rows, first_ref, second_ref, block):
    count = len(rows)
    width = rows[0].shape[-1]
    slot = lanes_of(rows[0].shape) // SLOT
    first = second = None
    for i, row in enumerate(rows):
        turned = pltpu.roll(row, SLOT * i, 1) if i else row
        first = turned if first is None else jnp.where(slot == i, turned, first)
        second = turned if second is None else jnp.where(slot == (i - 1) % count, turned, second)
    first_ref[block] = first.astype(BF16)
    second_ref[block] = second.astype(BF16)


def ring_row(main, right, left, i):
    width = main.shape[-1]
    lane = lanes_of(main.shape)
    both = jnp.where(lane // SLOT == i, right.astype(F32), left.astype(F32))
    if i:
        both = pltpu.roll(both, width - SLOT * i, 1)
    edge = jnp.where((lane < MARGIN) | (lane >= width - MARGIN), both, 0.0)
    return jnp.concatenate([main, edge.astype(BF16)], axis=1)


def build_ring(top_ref, main_ref, right_ref, left_ref, bottom_ref, ring_ref):
    size = main_ref.shape[0]
    per = main_ref.shape[-1] // SLOT
    shift = (-MARGIN) % per
    near = (MARGIN + per - 1) // per
    for e in range(MARGIN):
        block, slot = divmod(e + shift, per)
        ring_ref[e] = ring_row(
            top_ref[e], top_ref[MARGIN + block], top_ref[MARGIN + near + block], slot
        )
        block, slot = divmod(e, per)
        ring_ref[MARGIN + size + e] = ring_row(
            bottom_ref[e], bottom_ref[MARGIN + block], bottom_ref[MARGIN + near + block], slot
        )

    @pl.loop(0, size // per)
    def _(block):
        right = right_ref[block]
        left = left_ref[block]
        for slot in range(per):
            row = block * per + slot
            ring_ref[MARGIN + row] = ring_row(main_ref[row], right, left, slot)


def taps(row, spacing, width):
    wide = row.astype(F32)
    full = row.shape[-1]
    back = pltpu.roll(wide, spacing, 1)[:, :width]
    ahead = pltpu.roll(wide, full - spacing, 1)[:, :width]
    return jnp.concatenate([back.astype(BF16), row[:, :width], ahead.astype(BF16)], axis=0)


def wide_conv(source_ref, weights, spacing, sums_ref, finish, unroll):
    rows, channels, full = source_ref.shape

    def step(e, last):
        z = jnp.dot(weights, taps(source_ref[e], spacing, full), preferred_element_type=F32)
        if last:
            finish(e - 2 * spacing, sums_ref[e] + z[2 * channels :])
        sums_ref[e + spacing] += z[channels : 2 * channels]
        sums_ref[e + 2 * spacing] = z[:channels]

    run(rows, spacing, step, unroll)


def run(rows, spacing, step, unroll):
    @pl.loop(0, 2 * spacing, step=unroll)
    def _(e):
        for k in range(unroll):
            step(e + k, False)

    @pl.loop(2 * spacing, rows, step=unroll)
    def _(e):
        for k in range(unroll):
            step(e + k, True)


def narrow_conv(source_ref, weights, spacing, sums_ref, finish, unroll):
    rows, channels, full = source_ref.shape
    width = full // 2

    def step(half, last):
        e = 2 * half
        both = jnp.concatenate(
            [taps(source_ref[e + k], spacing, width) for k in range(2)], axis=1
        )
        z = jnp.dot(weights, both, preferred_element_type=F32)
        if last:
            finish(half - spacing, sums_ref[half] + z[2 * channels :])
        sums_ref[half + spacing // 2] += z[channels : 2 * channels]
        sums_ref[half + spacing] = z[:channels]

    run(rows // 2, spacing // 2, step, unroll)


def prepare_kernel(x_ref, xt_ref, first_ref, second_ref):
    channels, size, width = x_ref.shape
    per = width // SLOT

    @pl.loop(0, size // per)
    def _(block):
        chunk = x_ref[:, pl.ds(block * per, per), :].astype(F32)
        turned = jnp.swapaxes(chunk, 0, 1)
        xt_ref[pl.ds(block * per, per)] = turned.astype(BF16)
        pack_edges([turned[i] for i in range(per)], first_ref, second_ref, block)


def forward_kernel(
    place_ref, top_ref, main_ref, right_ref, left_ref, bottom_ref, target_ref,
    w1_ref, b1_ref, w2_ref, b2_ref,
    hidden_ref, slope_one_ref, slope_two_ref, send_ref,
    ring_ref, hidden_ring_ref, sums_ref,
):
    size, channels, width = main_ref.shape
    d1, d2 = DILATION_FIRST, DILATION_SECOND
    build_ring(top_ref, main_ref, right_ref, left_ref, bottom_ref, ring_ref)
    col, row, cols, rows = (place_ref[k] for k in range(4))
    lane = lanes_of((1, 2 * width))
    q = jnp.where(lane < width + width // 2, lane, lane - 2 * width) + row * width
    lane_ok = jnp.where((q >= 0) & (q < rows * width), 1.0, 0.0)
    w1 = w1_ref[...]
    w2 = w2_ref[...]
    b1 = b1_ref[...]
    b2 = b2_ref[...]

    def finish_one(o, total):
        pre = total + ring_ref[o + d1].astype(F32) + b1
        decay = jnp.exp(jnp.minimum(pre, 0.0))
        up = pre > 0
        p = o - d2 + col * size
        ok = lane_ok * jnp.where((p >= 0) & (p < cols * size), 1.0, 0.0)
        hidden_ring_ref[o] = (jnp.where(up, pre, decay - 1.0) * ok).astype(BF16)
        slope_one_ref[o] = jnp.where(up, 1.0, decay) * ok

    wide_conv(ring_ref, w1, d1, sums_ref, finish_one, 4)

    group = width // size
    mine = lax.rem(col, group)
    low = lanes_of((channels // 2, width)) < size

    def send(p, hidden):
        lo, hi = hidden[: channels // 2], hidden[channels // 2 :]
        send_ref[mine, p] = jnp.where(low, lo, pltpu.roll(hi, size, 1)).astype(BF16)
        send_ref[1 - mine, p] = jnp.where(low, pltpu.roll(lo, size, 1), hi).astype(BF16)

    def finish_two(half, total):
        for k in range(2):
            p = 2 * half + k
            pre = (
                total[:, k * width : (k + 1) * width]
                + hidden_ring_ref[p + d2, :, :width].astype(F32)
                + b2
            )
            decay = jnp.exp(jnp.minimum(pre, 0.0))
            up = pre > 0
            hidden = jnp.where(up, pre, decay - 1.0)
            hidden_ref[p] = hidden.astype(BF16)
            slope_two_ref[p] = jnp.where(up, 1.0, decay)
            send(p, hidden)

    narrow_conv(hidden_ring_ref, w2, d2, sums_ref, finish_two, 4)
    label = target_ref[...].astype(F32)
    send(size, label)


def head_kernel(
    place_ref, received_a_ref, received_b_ref, hidden_ref, slope_two_ref, target_ref,
    weight_ref, weight_t_ref, bias_ref,
    delta_ref, first_ref, second_ref,
    wide_ref, turned_ref, target_t_ref,
):
    size, channels, width = hidden_ref.shape
    half = channels // 2
    group = width // size
    mine = lax.rem(place_ref[0], group)

    @pl.loop(0, size, step=8)
    def _(p):
        for k in range(8):
            wide_ref[pl.ds((mine * size + p + k) * half, half), :] = received_a_ref[p + k].astype(F32)
            wide_ref[pl.ds(((1 - mine) * size + p + k) * half, half), :] = received_b_ref[p + k].astype(F32)

    @pl.loop(0, half, step=2)
    def _(c):
        for k in range(2):
            page = wide_ref[pl.ds(c + k, width, stride=half), :]
            page = page.T
            turned_ref[pl.ds(c + k, size, stride=channels), :] = page[:size]
            turned_ref[pl.ds(c + k + half, size, stride=channels), :] = page[size:]

    label_a = received_a_ref[size].astype(F32)
    label_b = received_b_ref[size].astype(F32)
    by_place = [
        jnp.where(mine == 0, label_a, label_b),
        jnp.where(mine == 0, label_b, label_a),
    ]
    page = jnp.concatenate(
        [by_place[0], pltpu.roll(by_place[0], size, 1), by_place[1], pltpu.roll(by_place[1], size, 1)],
        axis=0,
    )
    target_t_ref[...] = page.T[:size].astype(jnp.int32)

    bins = weight_ref.shape[0]
    weight = weight_ref[...]
    weight_t = weight_t_ref[...]
    bias = bias_ref[...]
    bin_id = lax.broadcasted_iota(jnp.int32, (bins, 2 * width), 0)
    per = width // SLOT

    def pair(p):
        symmetric = jnp.concatenate(
            [
                (
                    hidden_ref[p + k].astype(F32)
                    + turned_ref[pl.ds((p + k) * channels, channels), :]
                ).astype(BF16)
                for k in range(2)
            ],
            axis=1,
        )
        logits = jnp.dot(weight, symmetric, preferred_element_type=F32) + bias
        top = jnp.max(logits, axis=0, keepdims=True)
        raised = jnp.exp(logits - top)
        probability = raised / jnp.sum(raised, axis=0, keepdims=True)
        labels = [
            jnp.concatenate([ref[pl.ds(p + k, 1), :] for k in range(2)], axis=1)
            for ref in (target_ref, target_t_ref)
        ]
        grads = [
            (probability - jnp.where(bin_id == label, 1.0, 0.0)).astype(BF16).astype(F32)
            for label in labels
        ]
        bins_sum = (grads[0] + grads[1]).astype(BF16)
        grad_two = jnp.dot(weight_t, bins_sum, preferred_element_type=F32)
        return [
            (grad_two[:, k * width : (k + 1) * width] * slope_two_ref[p + k]).astype(BF16)
            for k in range(2)
        ]

    @pl.loop(0, size // per)
    def _(block):
        deltas = []
        for k in range(0, per, 2):
            deltas += pair(block * per + k)
        for k in range(per):
            delta_ref[block * per + k] = deltas[k]
        pack_edges([d.astype(F32) for d in deltas], first_ref, second_ref, block)


def backward_kernel(
    top_ref, main_ref, right_ref, left_ref, bottom_ref, slope_one_ref, w2_ref, w1_ref,
    out_ref,
    ring_ref, delta_ring_ref, sums_ref,
):
    size, channels, width = main_ref.shape
    d1, d2 = DILATION_FIRST, DILATION_SECOND
    build_ring(top_ref, main_ref, right_ref, left_ref, bottom_ref, ring_ref)
    w2 = w2_ref[...]
    w1 = w1_ref[...]

    def finish_one(o, total):
        grad = total + ring_ref[o + d2].astype(F32)
        delta_ring_ref[o] = (grad * slope_one_ref[o + d2 - d1]).astype(BF16)

    wide_conv(ring_ref, w2, d2, sums_ref, finish_one, 4)

    def finish_two(half, total):
        for k in range(2):
            p = 2 * half + k
            out_ref[pl.ds(p, channels, stride=size), :] = (
                total[:, k * width : (k + 1) * width]
                + delta_ring_ref[p + d1, :, :width].astype(F32)
            )

    narrow_conv(delta_ring_ref, w1, d1, sums_ref, finish_two, 2)


def shifted(tensor, axis, step):
    count = lax.axis_size(axis)
    pairs = [(i, i + step) for i in range(count) if 0 <= i + step < count]
    return lax.ppermute(tensor, axis, pairs)


def halos(main, first, second):
    right = shifted(first, "row", -1)
    left = shifted(second, "row", 1)
    near = -(-MARGIN // (main.shape[-1] // SLOT))
    top = shifted(jnp.concatenate([main[-MARGIN:], right[-near:], left[-near:]]), "col", 1)
    bottom = shifted(jnp.concatenate([main[:MARGIN], right[:near], left[:near]]), "col", -1)
    return top, main, right, left, bottom


def mirror_pairs(step):
    col_count, row_count = lax.axis_size("col"), lax.axis_size("row")
    group = col_count // row_count
    return [
        (r * col_count + c, (c // group) * col_count + group * r + (c % group + step) % group)
        for c in range(col_count)
        for r in range(row_count)
    ]


def local(
    pair_features,
    first_block_kernel,
    first_block_bias,
    second_block_kernel,
    second_block_bias,
    head_weight,
    head_bias,
    target,
):
    channels, size, width = pair_features.shape
    d1, d2 = DILATION_FIRST, DILATION_SECOND
    per = width // SLOT
    place = jnp.stack(
        [
            lax.axis_index("col"), lax.axis_index("row"),
            jnp.int32(lax.axis_size("col")), jnp.int32(lax.axis_size("row")),
        ]
    ).astype(jnp.int32)

    def ahead(kernel):
        return kernel.transpose(0, 2, 1, 3).reshape(3 * channels, 3 * channels)

    def back(kernel):
        return kernel[::-1, ::-1].transpose(0, 3, 1, 2).reshape(3 * channels, 3 * channels)

    row_type = jax.ShapeDtypeStruct((size, channels, width), BF16)
    pack_type = jax.ShapeDtypeStruct((size // per, channels, width), BF16)
    prepared = pl.pallas_call(
        prepare_kernel,
        out_shape=(row_type, pack_type, pack_type),
        in_specs=[VMEM],
        out_specs=(VMEM,) * 3,
        compiler_params=params(24),
        name="prepare",
    )(pair_features)
    around = halos(*prepared)

    near_rows = size + 2 * d2
    wide_rows = size + 2 * MARGIN
    hidden, slope_one, slope_two, sent = pl.pallas_call(
        forward_kernel,
        out_shape=(
            row_type,
            jax.ShapeDtypeStruct((near_rows, channels, 2 * width), F32),
            jax.ShapeDtypeStruct((size, channels, width), F32),
            jax.ShapeDtypeStruct((2, size + 1, channels // 2, width), BF16),
        ),
        in_specs=[SMEM] + [VMEM] * 10,
        out_specs=(VMEM,) * 4,
        scratch_shapes=[
            pltpu.VMEM((wide_rows, channels, 2 * width), BF16),
            pltpu.VMEM((near_rows, channels, 2 * width), BF16),
            pltpu.VMEM((wide_rows + 2 * d2, channels, 2 * width), F32),
        ],
        compiler_params=params(48),
        name="forward",
    )(
        place, *around, target,
        ahead(first_block_kernel), first_block_bias[:, None],
        ahead(second_block_kernel), second_block_bias[:, None],
    )
    received = [lax.ppermute(sent[k], ("row", "col"), mirror_pairs(k)) for k in range(2)]

    bins = head_weight.shape[0]
    bins_up = -(-bins // 16) * 16
    weight = jnp.pad(head_weight, ((0, bins_up - bins), (0, 0)))
    bias = jnp.pad(head_bias, (0, bins_up - bins), constant_values=-jnp.inf)[:, None]
    delta = pl.pallas_call(
        head_kernel,
        out_shape=(row_type, pack_type, pack_type),
        in_specs=[SMEM] + [VMEM] * 8,
        out_specs=(VMEM,) * 3,
        scratch_shapes=[
            pltpu.VMEM((2 * size * channels // 2, width), F32),
            pltpu.VMEM((size * channels, width), F32),
            pltpu.VMEM((size, width), jnp.int32),
        ],
        compiler_params=params(32),
        name="head",
    )(place, *received, hidden, slope_two, target, weight, weight.T, bias)
    around = halos(*delta)

    out = pl.pallas_call(
        backward_kernel,
        out_shape=jax.ShapeDtypeStruct((channels * size, width), F32),
        in_specs=[VMEM] * 8,
        out_specs=VMEM,
        scratch_shapes=[
            pltpu.VMEM((wide_rows, channels, 2 * width), BF16),
            pltpu.VMEM((near_rows - 2 * d1, channels, 2 * width), BF16),
            pltpu.VMEM((wide_rows + 2 * d2, channels, 2 * width), F32),
        ],
        compiler_params=params(48),
        name="backward",
    )(*around, slope_one, back(second_block_kernel), back(first_block_kernel))
    return out.reshape(channels, size, width)


def solution(mesh):
    in_specs = (P(None, "col", "row"), P(), P(), P(), P(), P(), P(), P("col", "row"))
    out_specs = P(None, "col", "row")
    return jax.shard_map(local, mesh=mesh, in_specs=in_specs, out_specs=out_specs, check_vma=False)
```

```python
import jax
import jax.numpy as jnp
from jax import lax
from jax.experimental import pallas as pl
from jax.experimental.pallas import tpu as pltpu
from jax.sharding import PartitionSpec as P

DILATION_FIRST = 4
DILATION_SECOND = 8
MARGIN = DILATION_FIRST + DILATION_SECOND
SLOT = 16
F32 = jnp.float32
BF16 = jnp.bfloat16
VMEM = pl.BlockSpec(memory_space=pltpu.VMEM)
SMEM = pl.BlockSpec(memory_space=pltpu.SMEM)


def params(megabytes):
    return pltpu.CompilerParams(vmem_limit_bytes=megabytes << 20)


def lanes_of(shape):
    return lax.broadcasted_iota(jnp.int32, shape, len(shape) - 1)


def pack_edges(rows, first_ref, second_ref, block):
    count = len(rows)
    width = rows[0].shape[-1]
    slot = lanes_of(rows[0].shape) // SLOT
    first = second = None
    for i, row in enumerate(rows):
        turned = pltpu.roll(row, SLOT * i, 1) if i else row
        first = turned if first is None else jnp.where(slot == i, turned, first)
        second = turned if second is None else jnp.where(slot == (i - 1) % count, turned, second)
    first_ref[block] = first.astype(BF16)
    second_ref[block] = second.astype(BF16)


def ring_row(main, right, left, i):
    width = main.shape[-1]
    lane = lanes_of(main.shape)
    both = jnp.where(lane // SLOT == i, right.astype(F32), left.astype(F32))
    if i:
        both = pltpu.roll(both, width - SLOT * i, 1)
    edge = jnp.where((lane < MARGIN) | (lane >= width - MARGIN), both, 0.0)
    return jnp.concatenate([main, edge.astype(BF16)], axis=1)


def strip_ring(strip_ref, slots, ring_ref):
    per = ring_ref.shape[-1] // 2 // SLOT
    near = -(-MARGIN // per)
    for e in range(MARGIN):
        block, slot = divmod(e + slots, per)
        right, left = strip_ref[MARGIN + block], strip_ref[MARGIN + near + block]
        ring_ref[e] = ring_row(strip_ref[e], right, left, slot)


def main_ring(main_ref, right_ref, left_ref, ring_ref):
    per = main_ref.shape[-1] // SLOT

    @pl.loop(0, main_ref.shape[0] // per)
    def _(block):
        right = right_ref[block]
        left = left_ref[block]
        for slot in range(per):
            row = block * per + slot
            ring_ref[row] = ring_row(main_ref[row], right, left, slot)


def taps(row, spacing, width):
    wide = row.astype(F32)
    full = row.shape[-1]
    back = pltpu.roll(wide, spacing, 1)[:, :width]
    ahead = pltpu.roll(wide, full - spacing, 1)[:, :width]
    return jnp.concatenate([back.astype(BF16), row[:, :width], ahead.astype(BF16)], axis=0)


def wide_unit(source_ref, spacing):
    def unit(e):
        row = source_ref[e]
        return taps(row, spacing, row.shape[-1]), row.astype(F32)

    return unit


def narrow_unit(source_ref, spacing):
    width = source_ref.shape[-1] // 2

    def unit(e):
        rows = [source_ref[2 * e + k] for k in range(2)]
        both = jnp.concatenate([taps(row, spacing, width) for row in rows], axis=1)
        return both, jnp.concatenate([row[:, :width] for row in rows], axis=1).astype(F32)

    return unit


def inner_conv(unit, count, weights, reach, sums_ref, finish, unroll):
    channels = weights.shape[0] // 3

    def step(e, kind):
        seen, own = unit(e)
        z = jnp.dot(weights, seen, preferred_element_type=F32)
        middle, behind = z[channels : 2 * channels] + own, z[2 * channels :]
        if kind == 0:
            sums_ref[e] = behind
            sums_ref[e + reach] = middle
        else:
            total = sums_ref[e] + behind
            if kind == 1:
                sums_ref[e] = total
            else:
                finish(e - 2 * reach, total)
            sums_ref[e + reach] += middle
        sums_ref[e + 2 * reach] = z[:channels]

    for kind, begin, end in ((0, 0, reach), (1, reach, 2 * reach), (2, 2 * reach, count)):
        many = max(k for k in range(1, unroll + 1) if (end - begin) % k == 0)

        @pl.loop(begin, end, step=many)
        def _(e):
            for k in range(many):
                step(e + k, kind)


def keep_sums(sums_ref, count, reach, kept_ref):
    for k in range(2 * reach):
        kept_ref[0, k] = sums_ref[k]
        kept_ref[1, k] = sums_ref[count + k]


def edge_conv(unit, count, weights, reach, below, kept_ref, parts_ref, finish):
    channels = weights.shape[0] // 3
    for k in range(count):
        seen, own = unit(k)
        if below:
            taken = [t for t in range(3) if k + (2 - t) * reach < count]
        else:
            taken = [t for t in range(3) if k - t * reach >= 0]
        z = jnp.dot(
            weights[channels * taken[0] : channels * (taken[-1] + 1)],
            seen,
            preferred_element_type=F32,
        )
        for i, t in enumerate(taken):
            part = z[channels * i : channels * (i + 1)]
            parts_ref[k, t] = part + own if t == 1 else part
    for i in range(count):
        if below:
            total = parts_ref[i, 2]
            others = [(i - (2 - t) * reach, t) for t in range(2)]
            kept = i
        else:
            total = parts_ref[i, 0]
            others = [(i + t * reach, t) for t in (1, 2)]
            kept = i - count + 2 * reach
        for k, t in others:
            if 0 <= k < count:
                total = total + parts_ref[k, t]
        if 0 <= kept < 2 * reach:
            total = total + kept_ref[int(below), kept]
        finish(i, total)


def activated(pre):
    decay = jnp.exp(jnp.minimum(pre, 0.0))
    up = pre > 0
    return jnp.where(up, pre, decay - 1.0), jnp.where(up, 1.0, decay)


def lanes_inside(place_ref, width):
    lane = lanes_of((1, 2 * width))
    q = jnp.where(lane < width + width // 2, lane, lane - 2 * width) + place_ref[1] * width
    return jnp.where((q >= 0) & (q < place_ref[3] * width), 1.0, 0.0)


def put_piece(send_refs, mine, p, hidden):
    channels, width = hidden.shape
    lo, hi = hidden[: channels // 2], hidden[channels // 2 :]
    low = lanes_of(lo.shape) < width // 2
    first = jnp.where(low, lo, pltpu.roll(hi, width // 2, 1)).astype(BF16)
    second = jnp.where(low, pltpu.roll(lo, width // 2, 1), hi).astype(BF16)
    swap = mine == 1
    send_refs[0][p] = jnp.where(swap, second, first)
    send_refs[1][p] = jnp.where(swap, first, second)


def prepare_kernel(x_ref, xt_ref, first_ref, second_ref):
    channels, size, width = x_ref.shape
    per = width // SLOT

    @pl.loop(0, size // per)
    def _(block):
        chunk = x_ref[:, pl.ds(block * per, per), :].astype(F32)
        turned = jnp.swapaxes(chunk, 0, 1)
        xt_ref[pl.ds(block * per, per)] = turned.astype(BF16)
        pack_edges([turned[i] for i in range(per)], first_ref, second_ref, block)


def forward_inner_kernel(
    place_ref, main_ref, right_ref, left_ref, target_ref, w1_ref, b1_ref, w2_ref, b2_ref,
    kept_one_ref, kept_two_ref, hidden_ref, slope_one_ref, slope_two_ref, send_a_ref, send_b_ref,
    ring_ref, near_ref, sums_ref,
):
    size, channels, width = main_ref.shape
    d1, d2 = DILATION_FIRST, DILATION_SECOND
    main_ring(main_ref, right_ref, left_ref, ring_ref)
    lane_ok = lanes_inside(place_ref, width)
    mine = lax.rem(place_ref[0], width // size)
    b1 = b1_ref[...]
    b2 = b2_ref[...]

    def finish_one(i, total):
        hidden, slope = activated(total + b1)
        near_ref[i] = (hidden * lane_ok).astype(BF16)
        slope_one_ref[i] = slope * lane_ok

    inner_conv(wide_unit(ring_ref, d1), size, w1_ref[...], d1, sums_ref, finish_one, 8)
    keep_sums(sums_ref, size, d1, kept_one_ref)

    def finish_two(i, total):
        hidden, slope = activated(total + b2)
        for k in range(2):
            own = hidden[:, k * width : (k + 1) * width]
            hidden_ref[2 * i + k] = own.astype(BF16)
            slope_two_ref[2 * i + k] = slope[:, k * width : (k + 1) * width]
            put_piece((send_a_ref, send_b_ref), mine, 2 * i + k, own)

    count = near_ref.shape[0] // 2
    inner_conv(narrow_unit(near_ref, d2), count, w2_ref[...], d2 // 2, sums_ref, finish_two, 10)
    keep_sums(sums_ref, count, d2 // 2, kept_two_ref)
    put_piece((send_a_ref, send_b_ref), mine, size - 2 * MARGIN, target_ref[...].astype(F32))


def forward_edge_kernel(
    place_ref, top_ref, bottom_ref, kept_one_ref, kept_two_ref, w1_ref, b1_ref, w2_ref, b2_ref,
    hidden_ref, slope_one_ref, slope_two_ref, send_a_ref, send_b_ref,
    ring_ref, near_ref, parts_ref,
):
    width = hidden_ref.shape[-1]
    size = width // 2
    d1, d2 = DILATION_FIRST, DILATION_SECOND
    lane_ok = lanes_inside(place_ref, width)
    mine = lax.rem(place_ref[0], width // size)
    b1 = b1_ref[...]
    b2 = b2_ref[...]
    w1 = w1_ref[...]
    w2 = w2_ref[...]
    for below, strip_ref in enumerate((top_ref, bottom_ref)):
        ring, near = ring_ref.at[below], near_ref.at[below]
        parts = parts_ref.at[below]
        strip_ring(strip_ref, 0 if below else -MARGIN % (width // SLOT), ring)

        def finish_one(i, total):
            hidden, slope = activated(total + b1)
            p = (size - d1 if below else d1 - MARGIN) + i + place_ref[0] * size
            ok = lane_ok * jnp.where((p >= 0) & (p < place_ref[2] * size), 1.0, 0.0)
            near[i] = (hidden * ok).astype(BF16)
            slope_one_ref[below, i] = slope * ok

        edge_conv(
            wide_unit(ring, d1), MARGIN, w1, d1, below, kept_one_ref, parts, finish_one
        )

        def finish_two(i, total):
            hidden, slope = activated(total + b2)
            for k in range(2):
                row = below * MARGIN + 2 * i + k
                own = hidden[:, k * width : (k + 1) * width]
                hidden_ref[row] = own.astype(BF16)
                slope_two_ref[row] = slope[:, k * width : (k + 1) * width]
                put_piece((send_a_ref, send_b_ref), mine, row, own)

        edge_conv(
            narrow_unit(near, d2), MARGIN // 2, w2, d2 // 2, below, kept_two_ref, parts, finish_two
        )


def head_kernel(
    place_ref, inner_a_ref, inner_b_ref, edge_a_ref, edge_b_ref,
    hidden_inner_ref, hidden_edge_ref, slope_inner_ref, slope_edge_ref, target_ref,
    weight_ref, weight_t_ref, bias_ref,
    delta_ref, first_ref, second_ref,
    wide_ref, turned_ref, target_t_ref,
):
    size, channels, width = delta_ref.shape
    half = channels // 2
    group = width // size
    mine = lax.rem(place_ref[0], group)
    inner = size - 2 * MARGIN

    def widen(source_a_ref, source_b_ref, row, p):
        wide_ref[pl.ds((mine * size + p) * half, half), :] = source_a_ref[row].astype(F32)
        wide_ref[pl.ds(((1 - mine) * size + p) * half, half), :] = source_b_ref[row].astype(F32)

    for k in range(inner):
        widen(inner_a_ref, inner_b_ref, k, k + MARGIN)
    for k in range(MARGIN):
        widen(edge_a_ref, edge_b_ref, k, k)
        widen(edge_a_ref, edge_b_ref, MARGIN + k, MARGIN + inner + k)

    @pl.loop(0, half, step=8)
    def _(c):
        for k in range(8):
            page = wide_ref[pl.ds(c + k, width, stride=half), :]
            page = page.T
            turned_ref[pl.ds(c + k, size, stride=channels), :] = page[:size]
            turned_ref[pl.ds(c + k + half, size, stride=channels), :] = page[size:]

    label_a = inner_a_ref[inner].astype(F32)
    label_b = inner_b_ref[inner].astype(F32)
    label_0 = jnp.where(mine == 0, label_a, label_b)
    label_1 = jnp.where(mine == 0, label_b, label_a)
    page = jnp.concatenate(
        [label_0, pltpu.roll(label_0, size, 1), label_1, pltpu.roll(label_1, size, 1)], axis=0
    )
    target_t_ref[...] = page.T[:size].astype(jnp.int32)

    bins = weight_ref.shape[0]
    weight = weight_ref[...]
    weight_t = weight_t_ref[...]
    bias = bias_ref[...]
    bin_id = lax.broadcasted_iota(jnp.int32, (bins, 2 * width), 0)
    per = width // SLOT

    def own(p, inner_ref, edge_ref):
        if p < MARGIN:
            return edge_ref[p]
        return inner_ref[p - MARGIN] if p < MARGIN + inner else edge_ref[p - inner]

    def pair(p):
        symmetric = jnp.concatenate(
            [
                (
                    own(p + k, hidden_inner_ref, hidden_edge_ref).astype(F32)
                    + turned_ref[pl.ds((p + k) * channels, channels), :]
                ).astype(BF16)
                for k in range(2)
            ],
            axis=1,
        )
        logits = jnp.dot(weight, symmetric, preferred_element_type=F32) + bias
        top = jnp.max(logits, axis=0, keepdims=True)
        raised = jnp.exp(logits - top)
        probability = raised / jnp.sum(raised, axis=0, keepdims=True)
        labels = [
            jnp.concatenate([ref[pl.ds(p + k, 1), :] for k in range(2)], axis=1)
            for ref in (target_ref, target_t_ref)
        ]
        grads = [
            (probability - jnp.where(bin_id == label, 1.0, 0.0)).astype(BF16).astype(F32)
            for label in labels
        ]
        bins_sum = (grads[0] + grads[1]).astype(BF16)
        grad_two = jnp.dot(weight_t, bins_sum, preferred_element_type=F32)
        return [
            (
                grad_two[:, k * width : (k + 1) * width]
                * own(p + k, slope_inner_ref, slope_edge_ref)
            ).astype(BF16)
            for k in range(2)
        ]

    for block in range(size // per):
        deltas = []
        for k in range(0, per, 2):
            deltas += pair(block * per + k)
        for k in range(per):
            delta_ref[block * per + k] = deltas[k]
        pack_edges([d.astype(F32) for d in deltas], first_ref, second_ref, block)


def backward_inner_kernel(
    main_ref, right_ref, left_ref, slope_one_ref, w2_ref, w1_ref,
    kept_two_ref, kept_one_ref, rows_ref,
    ring_ref, near_ref, sums_ref,
):
    size, channels, width = main_ref.shape
    d1, d2 = DILATION_FIRST, DILATION_SECOND
    main_ring(main_ref, right_ref, left_ref, ring_ref)

    def finish_one(i, total):
        near_ref[i] = (total * slope_one_ref[i + d2 - d1]).astype(BF16)

    inner_conv(wide_unit(ring_ref, d2), size, w2_ref[...], d2, sums_ref, finish_one, 8)
    keep_sums(sums_ref, size, d2, kept_two_ref)

    def finish_two(i, total):
        for k in range(2):
            rows_ref[2 * i + k] = total[:, k * width : (k + 1) * width]

    count = near_ref.shape[0] // 2
    inner_conv(narrow_unit(near_ref, d1), count, w1_ref[...], d1 // 2, sums_ref, finish_two, 10)
    keep_sums(sums_ref, count, d1 // 2, kept_one_ref)


def backward_edge_kernel(
    top_ref, bottom_ref, kept_two_ref, kept_one_ref, rows_ref, slope_inner_ref, slope_edge_ref,
    w2_ref, w1_ref,
    out_ref,
    ring_ref, near_ref, parts_ref,
):
    inner, channels, width = rows_ref.shape
    size = inner + 2 * MARGIN
    d1, d2 = DILATION_FIRST, DILATION_SECOND
    w2 = w2_ref[...]
    w1 = w1_ref[...]

    def put(p, row):
        out_ref[pl.ds(p, channels, stride=size), :] = row

    for k in range(inner):
        put(k + MARGIN, rows_ref[k])
    for below, strip_ref in enumerate((top_ref, bottom_ref)):
        ring, near = ring_ref.at[below], near_ref.at[below]
        parts = parts_ref.at[below]
        strip_ring(strip_ref, 0 if below else -MARGIN % (width // SLOT), ring)

        def finish_one(i, total):
            p = (size - d2 if below else d2 - MARGIN) + i
            if d1 <= p < size - d1:
                slope = slope_inner_ref[p - d1]
            else:
                slope = slope_edge_ref[below, p - (size - d1 if below else d1 - MARGIN)]
            near[i] = (total * slope).astype(BF16)

        edge_conv(
            wide_unit(ring, d2), MARGIN, w2, d2, below, kept_two_ref, parts, finish_one
        )

        def finish_two(i, total):
            for k in range(2):
                p = below * (size - MARGIN) + 2 * i + k
                put(p, total[:, k * width : (k + 1) * width])

        edge_conv(
            narrow_unit(near, d1), MARGIN // 2, w1, d1 // 2, below, kept_one_ref, parts, finish_two
        )


def shifted(tensor, axis, step):
    count = lax.axis_size(axis)
    pairs = [(i, i + step) for i in range(count) if 0 <= i + step < count]
    return lax.ppermute(tensor, axis, pairs)


def strips(main, right, left):
    near = -(-MARGIN // (main.shape[-1] // SLOT))
    top = shifted(jnp.concatenate([main[-MARGIN:], right[-near:], left[-near:]]), "col", 1)
    bottom = shifted(jnp.concatenate([main[:MARGIN], right[:near], left[:near]]), "col", -1)
    return top, bottom


def mirror_pairs(step):
    col_count, row_count = lax.axis_size("col"), lax.axis_size("row")
    group = col_count // row_count
    return [
        (r * col_count + c, (c // group) * col_count + group * r + (c % group + step) % group)
        for c in range(col_count)
        for r in range(row_count)
    ]


def local(
    pair_features,
    first_block_kernel,
    first_block_bias,
    second_block_kernel,
    second_block_bias,
    head_weight,
    head_bias,
    target,
):
    channels, size, width = pair_features.shape
    d1, d2 = DILATION_FIRST, DILATION_SECOND
    per = width // SLOT
    place = jnp.stack(
        [
            lax.axis_index("col"), lax.axis_index("row"),
            jnp.int32(lax.axis_size("col")), jnp.int32(lax.axis_size("row")),
        ]
    ).astype(jnp.int32)

    def ahead(kernel):
        return kernel.transpose(0, 2, 1, 3).reshape(3 * channels, 3 * channels)

    def back(kernel):
        return kernel[::-1, ::-1].transpose(0, 3, 1, 2).reshape(3 * channels, 3 * channels)

    def rows(count, lanes=width, kind=BF16):
        return jax.ShapeDtypeStruct((count, channels, lanes), kind)

    def sides(count, lanes=2 * width):
        return jax.ShapeDtypeStruct((2, count, channels, lanes), F32)

    def pieces(count):
        return jax.ShapeDtypeStruct((count, channels // 2, width), BF16)

    def call(kernel, name, outs, scratch, megabytes, flops, *operands):
        places = [SMEM if operand is place else VMEM for operand in operands]
        return pl.pallas_call(
            kernel,
            out_shape=outs,
            in_specs=places,
            out_specs=jax.tree.map(lambda _: VMEM, outs),
            scratch_shapes=[pltpu.VMEM(shape, kind) for shape, kind in scratch],
            compiler_params=params(megabytes),
            cost_estimate=pl.CostEstimate(flops=flops, bytes_accessed=8 << 20, transcendentals=0),
            name=name,
        )(*operands)

    inner = size - 2 * MARGIN
    ring = (channels, 2 * width)
    parts = ((2, MARGIN, 3) + ring, F32)
    edge_rings = [((2, MARGIN) + ring, BF16), ((2, MARGIN) + ring, BF16), parts]
    macs = 9 * channels * channels * size * width

    packs = rows(size // per)
    main, first, second = call(
        prepare_kernel, "prepare", (rows(size), packs, packs), [], 24, 1, pair_features
    )
    right, left = shifted(first, "row", -1), shifted(second, "row", 1)
    top, bottom = strips(main, right, left)
    w1, w2 = ahead(first_block_kernel), ahead(second_block_kernel)
    b1, b2 = first_block_bias[:, None], second_block_bias[:, None]
    kept_one, kept_two, hidden_inner, slope_one_inner, slope_two_inner, *sent_inner = call(
        forward_inner_kernel,
        "forward_inner",
        (
            sides(2 * d1), sides(d2), rows(inner), rows(size - 2 * d1, 2 * width, F32),
            rows(inner, width, F32), pieces(inner + 1), pieces(inner + 1),
        ),
        [
            ((size,) + ring, BF16), ((size - 2 * d1,) + ring, BF16),
            ((size + 2 * d1,) + ring, F32),
        ],
        32, 8 * macs, place, main, right, left, target, w1, b1, w2, b2,
    )
    got_inner = [lax.ppermute(sent_inner[k], ("row", "col"), mirror_pairs(k)) for k in range(2)]
    hidden_edge, slope_one_edge, slope_two_edge, *sent_edge = call(
        forward_edge_kernel,
        "forward_edge",
        (
            rows(2 * MARGIN), sides(MARGIN), rows(2 * MARGIN, width, F32),
            pieces(2 * MARGIN), pieces(2 * MARGIN),
        ),
        edge_rings,
        32, 4 * macs, place, top, bottom, kept_one, kept_two, w1, b1, w2, b2,
    )
    got_edge = [lax.ppermute(sent_edge[k], ("row", "col"), mirror_pairs(k)) for k in range(2)]

    bins = head_weight.shape[0]
    bins_up = -(-bins // 16) * 16
    weight = jnp.pad(head_weight, ((0, bins_up - bins), (0, 0)))
    bias = jnp.pad(head_bias, (0, bins_up - bins), constant_values=-jnp.inf)[:, None]
    delta, first, second = call(
        head_kernel,
        "head",
        (rows(size), packs, packs),
        [
            ((width * channels // 2, width), F32), ((size * channels, width), F32),
            ((size, width), jnp.int32),
        ],
        24, 4 * macs, place, *got_inner, *got_edge, hidden_inner, hidden_edge,
        slope_two_inner, slope_two_edge, target, weight, weight.T, bias,
    )
    right, left = shifted(first, "row", -1), shifted(second, "row", 1)
    top, bottom = strips(delta, right, left)
    w1, w2 = back(first_block_kernel), back(second_block_kernel)
    kept_two, kept_one, inner_rows = call(
        backward_inner_kernel,
        "backward_inner",
        (sides(2 * d2), sides(d1), rows(inner, width, F32)),
        [
            ((size,) + ring, BF16), ((size - 2 * d2,) + ring, BF16),
            ((size + 2 * d2,) + ring, F32),
        ],
        32, 8 * macs, delta, right, left, slope_one_inner, w2, w1,
    )
    out = call(
        backward_edge_kernel,
        "backward_edge",
        jax.ShapeDtypeStruct((channels * size, width), F32),
        edge_rings,
        32, 4 * macs, top, bottom, kept_two, kept_one, inner_rows,
        slope_one_inner, slope_one_edge, w2, w1,
    )
    return out.reshape(channels, size, width)


def solution(mesh):
    in_specs = (P(None, "col", "row"), P(), P(), P(), P(), P(), P(), P("col", "row"))
    out_specs = P(None, "col", "row")
    return jax.shard_map(local, mesh=mesh, in_specs=in_specs, out_specs=out_specs, check_vma=False)
```

```python
import jax
import jax.numpy as jnp
from jax import lax
from jax.experimental import pallas as pl
from jax.experimental.pallas import tpu as pltpu
from jax.sharding import PartitionSpec as P

DILATION_FIRST = 4
DILATION_SECOND = 8
MARGIN = DILATION_FIRST + DILATION_SECOND
SLOT = 16
F32 = jnp.float32
BF16 = jnp.bfloat16
VMEM = pl.BlockSpec(memory_space=pltpu.VMEM)


def params(megabytes):
    return pltpu.CompilerParams(vmem_limit_bytes=megabytes << 20)


def lanes_of(shape):
    return lax.broadcasted_iota(jnp.int32, shape, len(shape) - 1)


def pack_edges(rows, first_ref, second_ref, block):
    count = len(rows)
    width = rows[0].shape[-1]
    slot = lanes_of(rows[0].shape) // SLOT
    first = second = None
    for i, row in enumerate(rows):
        turned = pltpu.roll(row, SLOT * i, 1) if i else row
        first = turned if first is None else jnp.where(slot == i, turned, first)
        second = turned if second is None else jnp.where(slot == (i - 1) % count, turned, second)
    first_ref[block] = first.astype(BF16)
    second_ref[block] = second.astype(BF16)


def ring_row(main, right, left, i):
    width = main.shape[-1]
    lane = lanes_of(main.shape)
    both = jnp.where(lane // SLOT == i, right.astype(F32), left.astype(F32))
    if i:
        both = pltpu.roll(both, width - SLOT * i, 1)
    edge = jnp.where((lane < MARGIN) | (lane >= width - MARGIN), both, 0.0)
    return jnp.concatenate([main, edge.astype(BF16)], axis=1)


def strip_ring(strip_ref, slots, ring_ref):
    per = ring_ref.shape[-1] // 2 // SLOT
    near = -(-MARGIN // per)
    for e in range(MARGIN):
        block, slot = divmod(e + slots, per)
        right, left = strip_ref[MARGIN + block], strip_ref[MARGIN + near + block]
        ring_ref[e] = ring_row(strip_ref[e], right, left, slot)


def main_ring(main_ref, right_ref, left_ref, ring_ref):
    per = main_ref.shape[-1] // SLOT

    @pl.loop(0, main_ref.shape[0] // per)
    def _(block):
        right = right_ref[block]
        left = left_ref[block]
        for slot in range(per):
            row = block * per + slot
            ring_ref[row] = ring_row(main_ref[row], right, left, slot)


def taps(row, spacing, width):
    wide = row.astype(F32)
    full = row.shape[-1]
    back = pltpu.roll(wide, spacing, 1)[:, :width]
    ahead = pltpu.roll(wide, full - spacing, 1)[:, :width]
    return jnp.concatenate([back.astype(BF16), row[:, :width], ahead.astype(BF16)], axis=0)


def wide_unit(source_ref, spacing):
    def unit(e):
        row = source_ref[e]
        return taps(row, spacing, row.shape[-1]), row.astype(F32)

    return unit


def narrow_unit(source_ref, spacing):
    width = source_ref.shape[-1] // 2

    def unit(e):
        rows = [source_ref[2 * e + k] for k in range(2)]
        both = jnp.concatenate([taps(row, spacing, width) for row in rows], axis=1)
        return both, jnp.concatenate([row[:, :width] for row in rows], axis=1).astype(F32)

    return unit


def inner_conv(unit, count, weights, reach, sums_ref, finish, unroll):
    channels = weights.shape[0] // 3

    def step(e, kind):
        seen, own = unit(e)
        z = jnp.dot(weights, seen, preferred_element_type=F32)
        middle, behind = z[channels : 2 * channels] + own, z[2 * channels :]
        if kind == 0:
            sums_ref[e] = behind
            sums_ref[e + reach] = middle
        else:
            total = sums_ref[e] + behind
            if kind == 1:
                sums_ref[e] = total
            else:
                finish(e - 2 * reach, total)
            sums_ref[e + reach] += middle
        sums_ref[e + 2 * reach] = z[:channels]

    for kind, begin, end in ((0, 0, reach), (1, reach, 2 * reach), (2, 2 * reach, count)):
        many = max(k for k in range(1, unroll + 1) if (end - begin) % k == 0)

        @pl.loop(begin, end, step=many)
        def _(e):
            for k in range(many):
                step(e + k, kind)


def keep_sums(sums_ref, count, reach, kept_ref):
    for k in range(2 * reach):
        kept_ref[0, k] = sums_ref[k]
        kept_ref[1, k] = sums_ref[count + k]


def edge_conv(unit, count, weights, reach, below, kept_ref, parts_ref, finish):
    channels = weights.shape[0] // 3
    for k in range(count):
        seen, own = unit(k)
        if below:
            taken = [t for t in range(3) if k + (2 - t) * reach < count]
        else:
            taken = [t for t in range(3) if k - t * reach >= 0]
        z = jnp.dot(
            weights[channels * taken[0] : channels * (taken[-1] + 1)],
            seen,
            preferred_element_type=F32,
        )
        for i, t in enumerate(taken):
            part = z[channels * i : channels * (i + 1)]
            parts_ref[k, t] = part + own if t == 1 else part
    for i in range(count):
        if below:
            total = parts_ref[i, 2]
            others = [(i - (2 - t) * reach, t) for t in range(2)]
            kept = i
        else:
            total = parts_ref[i, 0]
            others = [(i + t * reach, t) for t in (1, 2)]
            kept = i - count + 2 * reach
        for k, t in others:
            if 0 <= k < count:
                total = total + parts_ref[k, t]
        if 0 <= kept < 2 * reach:
            total = total + kept_ref[int(below), kept]
        finish(i, total)


def activated(pre):
    decay = jnp.exp(jnp.minimum(pre, 0.0))
    up = pre > 0
    return jnp.where(up, pre, decay - 1.0), jnp.where(up, 1.0, decay)


def lanes_inside(width):
    lane = lanes_of((1, 2 * width))
    q = jnp.where(lane < width + width // 2, lane, lane - 2 * width) + lax.axis_index("row") * width
    return jnp.where((q >= 0) & (q < lax.axis_size("row") * width), 1.0, 0.0)


def put_piece(send_refs, mine, p, hidden):
    channels, width = hidden.shape
    lo, hi = hidden[: channels // 2], hidden[channels // 2 :]
    low = lanes_of(lo.shape) < width // 2
    first = jnp.where(low, lo, pltpu.roll(hi, width // 2, 1)).astype(BF16)
    second = jnp.where(low, pltpu.roll(lo, width // 2, 1), hi).astype(BF16)
    swap = mine == 1
    send_refs[0][p] = jnp.where(swap, second, first)
    send_refs[1][p] = jnp.where(swap, first, second)


def prepare_kernel(x_ref, xt_ref, first_ref, second_ref):
    channels, size, width = x_ref.shape
    per = width // SLOT

    @pl.loop(0, size // per)
    def _(block):
        chunk = x_ref[:, pl.ds(block * per, per), :].astype(F32)
        turned = jnp.swapaxes(chunk, 0, 1)
        xt_ref[pl.ds(block * per, per)] = turned.astype(BF16)
        pack_edges([turned[i] for i in range(per)], first_ref, second_ref, block)


def weights_kernel(
    k1_ref, k2_ref, b1_ref, b2_ref, head_ref, head_bias_ref,
    ahead_1_ref, ahead_2_ref, back_1_ref, back_2_ref,
    column_1_ref, column_2_ref, head_up_ref, head_t_ref, head_column_ref,
    scratch_ref,
):
    for kernel_ref, ahead_ref, back_ref in (
        (k1_ref, ahead_1_ref, back_1_ref), (k2_ref, ahead_2_ref, back_2_ref)
    ):
        taps = [[kernel_ref[t, s].astype(F32) for s in range(3)] for t in range(3)]
        ahead = [jnp.concatenate(taps[t], axis=1) for t in range(3)]
        ahead_ref[...] = jnp.concatenate(ahead, axis=0).astype(BF16)
        back = [
            jnp.concatenate([taps[2 - t][2 - s].T for s in range(3)], axis=1) for t in range(3)
        ]
        back_ref[...] = jnp.concatenate(back, axis=0).astype(BF16)

    def column(row_ref):
        row = row_ref[...]
        return jnp.broadcast_to(row, (column_1_ref.shape[1], row.shape[1])).T

    column_1_ref[...] = column(b1_ref)
    column_2_ref[...] = column(b2_ref)
    bins = head_ref.shape[0]
    head_column_ref[...] = jnp.full(head_column_ref.shape, -jnp.inf, F32)
    head_column_ref[:bins] = column(head_bias_ref)
    scratch_ref[...] = jnp.zeros(scratch_ref.shape, F32)
    scratch_ref[:bins] = head_ref[...].astype(F32)
    head_up_ref[...] = scratch_ref[...].astype(BF16)
    head_t_ref[...] = scratch_ref[...].T.astype(BF16)


def strips_kernel(main_ref, right_ref, left_ref, down_ref, up_ref):
    size = main_ref.shape[0]
    blocks = right_ref.shape[0]
    near = (down_ref.shape[0] - MARGIN) // 2
    for k in range(MARGIN):
        down_ref[k] = main_ref[size - MARGIN + k]
        up_ref[k] = main_ref[k]
    for k in range(near):
        down_ref[MARGIN + k] = right_ref[blocks - near + k]
        down_ref[MARGIN + near + k] = left_ref[blocks - near + k]
        up_ref[MARGIN + k] = right_ref[k]
        up_ref[MARGIN + near + k] = left_ref[k]


def forward_inner_kernel(
    main_ref, right_ref, left_ref, target_ref, w1_ref, b1_ref, w2_ref, b2_ref,
    kept_one_ref, kept_two_ref, hidden_ref, slope_one_ref, slope_two_ref, send_a_ref, send_b_ref,
    ring_ref, near_ref, sums_ref,
):
    size, channels, width = main_ref.shape
    d1, d2 = DILATION_FIRST, DILATION_SECOND
    main_ring(main_ref, right_ref, left_ref, ring_ref)
    lane_ok = lanes_inside(width)
    mine = lax.rem(lax.axis_index("col"), width // size)
    b1 = jnp.concatenate([b1_ref[...]] * 2, axis=1)
    b2 = jnp.concatenate([b2_ref[...]] * 2, axis=1)

    def finish_one(i, total):
        hidden, slope = activated(total + b1)
        near_ref[i] = (hidden * lane_ok).astype(BF16)
        slope_one_ref[i] = slope * lane_ok

    inner_conv(wide_unit(ring_ref, d1), size, w1_ref[...], d1, sums_ref, finish_one, 8)
    keep_sums(sums_ref, size, d1, kept_one_ref)

    def finish_two(i, total):
        hidden, slope = activated(total + b2)
        for k in range(2):
            own = hidden[:, k * width : (k + 1) * width]
            hidden_ref[2 * i + k] = own.astype(BF16)
            slope_two_ref[2 * i + k] = slope[:, k * width : (k + 1) * width]
            put_piece((send_a_ref, send_b_ref), mine, 2 * i + k, own)

    count = near_ref.shape[0] // 2
    inner_conv(narrow_unit(near_ref, d2), count, w2_ref[...], d2 // 2, sums_ref, finish_two, 10)
    keep_sums(sums_ref, count, d2 // 2, kept_two_ref)
    put_piece((send_a_ref, send_b_ref), mine, size - 2 * MARGIN, target_ref[...].astype(F32))


def forward_edge_kernel(
    top_ref, bottom_ref, kept_one_ref, kept_two_ref, w1_ref, b1_ref, w2_ref, b2_ref,
    hidden_ref, slope_one_ref, slope_two_ref, send_a_ref, send_b_ref,
    ring_ref, near_ref, parts_ref,
):
    width = hidden_ref.shape[-1]
    size = width // 2
    d1, d2 = DILATION_FIRST, DILATION_SECOND
    lane_ok = lanes_inside(width)
    mine = lax.rem(lax.axis_index("col"), width // size)
    b1 = jnp.concatenate([b1_ref[...]] * 2, axis=1)
    b2 = jnp.concatenate([b2_ref[...]] * 2, axis=1)
    w1 = w1_ref[...]
    w2 = w2_ref[...]
    for below, strip_ref in enumerate((top_ref, bottom_ref)):
        ring, near = ring_ref.at[below], near_ref.at[below]
        parts = parts_ref.at[below]
        strip_ring(strip_ref, 0 if below else -MARGIN % (width // SLOT), ring)

        def finish_one(i, total):
            hidden, slope = activated(total + b1)
            p = (size - d1 if below else d1 - MARGIN) + i + lax.axis_index("col") * size
            ok = lane_ok * jnp.where((p >= 0) & (p < lax.axis_size("col") * size), 1.0, 0.0)
            near[i] = (hidden * ok).astype(BF16)
            slope_one_ref[below, i] = slope * ok

        edge_conv(
            wide_unit(ring, d1), MARGIN, w1, d1, below, kept_one_ref, parts, finish_one
        )

        def finish_two(i, total):
            hidden, slope = activated(total + b2)
            for k in range(2):
                row = below * MARGIN + 2 * i + k
                own = hidden[:, k * width : (k + 1) * width]
                hidden_ref[row] = own.astype(BF16)
                slope_two_ref[row] = slope[:, k * width : (k + 1) * width]
                put_piece((send_a_ref, send_b_ref), mine, row, own)

        edge_conv(
            narrow_unit(near, d2), MARGIN // 2, w2, d2 // 2, below, kept_two_ref, parts, finish_two
        )


def head_kernel(
    inner_a_ref, inner_b_ref, edge_a_ref, edge_b_ref,
    hidden_inner_ref, hidden_edge_ref, slope_inner_ref, slope_edge_ref, target_ref,
    weight_ref, weight_t_ref, bias_ref,
    delta_ref, first_ref, second_ref,
    wide_ref, turned_ref, target_t_ref,
):
    size, channels, width = delta_ref.shape
    half = channels // 2
    group = width // size
    mine = lax.rem(lax.axis_index("col"), group)
    inner = size - 2 * MARGIN

    def widen(source_a_ref, source_b_ref, row, p):
        wide_ref[pl.ds((mine * size + p) * half, half), :] = source_a_ref[row].astype(F32)
        wide_ref[pl.ds(((1 - mine) * size + p) * half, half), :] = source_b_ref[row].astype(F32)

    for k in range(inner):
        widen(inner_a_ref, inner_b_ref, k, k + MARGIN)
    for k in range(MARGIN):
        widen(edge_a_ref, edge_b_ref, k, k)
        widen(edge_a_ref, edge_b_ref, MARGIN + k, MARGIN + inner + k)

    @pl.loop(0, half, step=8)
    def _(c):
        for k in range(8):
            page = wide_ref[pl.ds(c + k, width, stride=half), :]
            page = page.T
            turned_ref[pl.ds(c + k, size, stride=channels), :] = page[:size]
            turned_ref[pl.ds(c + k + half, size, stride=channels), :] = page[size:]

    label_a = inner_a_ref[inner].astype(F32)
    label_b = inner_b_ref[inner].astype(F32)
    label_0 = jnp.where(mine == 0, label_a, label_b)
    label_1 = jnp.where(mine == 0, label_b, label_a)
    page = jnp.concatenate(
        [label_0, pltpu.roll(label_0, size, 1), label_1, pltpu.roll(label_1, size, 1)], axis=0
    )
    target_t_ref[...] = page.T[:size].astype(jnp.int32)

    bins = weight_ref.shape[0]
    weight = weight_ref[...]
    weight_t = weight_t_ref[...]
    bias = jnp.concatenate([bias_ref[...]] * 2, axis=1)
    bin_id = lax.broadcasted_iota(jnp.int32, (bins, 2 * width), 0)
    per = width // SLOT

    def own(p, inner_ref, edge_ref):
        if p < MARGIN:
            return edge_ref[p]
        return inner_ref[p - MARGIN] if p < MARGIN + inner else edge_ref[p - inner]

    def pair(p):
        symmetric = jnp.concatenate(
            [
                (
                    own(p + k, hidden_inner_ref, hidden_edge_ref).astype(F32)
                    + turned_ref[pl.ds((p + k) * channels, channels), :]
                ).astype(BF16)
                for k in range(2)
            ],
            axis=1,
        )
        logits = jnp.dot(weight, symmetric, preferred_element_type=F32) + bias
        top = jnp.max(logits, axis=0, keepdims=True)
        raised = jnp.exp(logits - top)
        probability = raised / jnp.sum(raised, axis=0, keepdims=True)
        labels = [
            jnp.concatenate([ref[pl.ds(p + k, 1), :] for k in range(2)], axis=1)
            for ref in (target_ref, target_t_ref)
        ]
        grads = [
            (probability - jnp.where(bin_id == label, 1.0, 0.0)).astype(BF16).astype(F32)
            for label in labels
        ]
        bins_sum = (grads[0] + grads[1]).astype(BF16)
        grad_two = jnp.dot(weight_t, bins_sum, preferred_element_type=F32)
        return [
            (
                grad_two[:, k * width : (k + 1) * width]
                * own(p + k, slope_inner_ref, slope_edge_ref)
            ).astype(BF16)
            for k in range(2)
        ]

    for block in range(size // per):
        deltas = []
        for k in range(0, per, 2):
            deltas += pair(block * per + k)
        for k in range(per):
            delta_ref[block * per + k] = deltas[k]
        pack_edges([d.astype(F32) for d in deltas], first_ref, second_ref, block)


def backward_inner_kernel(
    main_ref, right_ref, left_ref, slope_one_ref, w2_ref, w1_ref,
    kept_two_ref, kept_one_ref, rows_ref,
    ring_ref, near_ref, sums_ref,
):
    size, channels, width = main_ref.shape
    d1, d2 = DILATION_FIRST, DILATION_SECOND
    main_ring(main_ref, right_ref, left_ref, ring_ref)

    def finish_one(i, total):
        near_ref[i] = (total * slope_one_ref[i + d2 - d1]).astype(BF16)

    inner_conv(wide_unit(ring_ref, d2), size, w2_ref[...], d2, sums_ref, finish_one, 8)
    keep_sums(sums_ref, size, d2, kept_two_ref)

    def finish_two(i, total):
        for k in range(2):
            rows_ref[2 * i + k] = total[:, k * width : (k + 1) * width]

    count = near_ref.shape[0] // 2
    inner_conv(narrow_unit(near_ref, d1), count, w1_ref[...], d1 // 2, sums_ref, finish_two, 10)
    keep_sums(sums_ref, count, d1 // 2, kept_one_ref)


def backward_edge_kernel(
    top_ref, bottom_ref, kept_two_ref, kept_one_ref, rows_ref, slope_inner_ref, slope_edge_ref,
    w2_ref, w1_ref,
    out_ref,
    ring_ref, near_ref, parts_ref,
):
    inner, channels, width = rows_ref.shape
    size = inner + 2 * MARGIN
    d1, d2 = DILATION_FIRST, DILATION_SECOND
    w2 = w2_ref[...]
    w1 = w1_ref[...]

    def put(p, row):
        out_ref[pl.ds(p, channels, stride=size), :] = row

    for k in range(inner):
        put(k + MARGIN, rows_ref[k])
    for below, strip_ref in enumerate((top_ref, bottom_ref)):
        ring, near = ring_ref.at[below], near_ref.at[below]
        parts = parts_ref.at[below]
        strip_ring(strip_ref, 0 if below else -MARGIN % (width // SLOT), ring)

        def finish_one(i, total):
            p = (size - d2 if below else d2 - MARGIN) + i
            if d1 <= p < size - d1:
                slope = slope_inner_ref[p - d1]
            else:
                slope = slope_edge_ref[below, p - (size - d1 if below else d1 - MARGIN)]
            near[i] = (total * slope).astype(BF16)

        edge_conv(
            wide_unit(ring, d2), MARGIN, w2, d2, below, kept_two_ref, parts, finish_one
        )

        def finish_two(i, total):
            for k in range(2):
                p = below * (size - MARGIN) + 2 * i + k
                put(p, total[:, k * width : (k + 1) * width])

        edge_conv(
            narrow_unit(near, d1), MARGIN // 2, w1, d1 // 2, below, kept_one_ref, parts, finish_two
        )


def shifted(tensor, axis, step):
    count = lax.axis_size(axis)
    pairs = [(i, i + step) for i in range(count) if 0 <= i + step < count]
    return lax.ppermute(tensor, axis, pairs)


def mirror_pairs(step):
    col_count, row_count = lax.axis_size("col"), lax.axis_size("row")
    group = col_count // row_count
    return [
        (r * col_count + c, (c // group) * col_count + group * r + (c % group + step) % group)
        for c in range(col_count)
        for r in range(row_count)
    ]


def local(
    pair_features,
    first_block_kernel,
    first_block_bias,
    second_block_kernel,
    second_block_bias,
    head_weight,
    head_bias,
    target,
):
    channels, size, width = pair_features.shape
    d1, d2 = DILATION_FIRST, DILATION_SECOND
    per = width // SLOT
    def rows(count, lanes=width, kind=BF16):
        return jax.ShapeDtypeStruct((count, channels, lanes), kind)

    def sides(count, lanes=2 * width):
        return jax.ShapeDtypeStruct((2, count, channels, lanes), F32)

    def pieces(count):
        return jax.ShapeDtypeStruct((count, channels // 2, width), BF16)

    def call(kernel, name, outs, scratch, megabytes, flops, *operands):
        return pl.pallas_call(
            kernel,
            out_shape=outs,
            in_specs=[VMEM] * len(operands),
            out_specs=jax.tree.map(lambda _: VMEM, outs),
            scratch_shapes=[pltpu.VMEM(shape, kind) for shape, kind in scratch],
            compiler_params=params(megabytes),
            cost_estimate=pl.CostEstimate(flops=flops, bytes_accessed=8 << 20, transcendentals=0),
            name=name,
        )(*operands)

    inner = size - 2 * MARGIN
    ring = (channels, 2 * width)
    parts = ((2, MARGIN, 3) + ring, F32)
    edge_rings = [((2, MARGIN) + ring, BF16), ((2, MARGIN) + ring, BF16), parts]
    macs = 9 * channels * channels * size * width

    packs = rows(size // per)
    square = jax.ShapeDtypeStruct((3 * channels, 3 * channels), BF16)
    bins = head_weight.shape[0]
    bins_up = -(-bins // 16) * 16
    column = jax.ShapeDtypeStruct((channels, width), F32)
    w1, w2, back_1, back_2, b1, b2, weight, weight_t, bias = call(
        weights_kernel,
        "weights",
        (square,) * 4 + (
            column, column, jax.ShapeDtypeStruct((bins_up, channels), BF16),
            jax.ShapeDtypeStruct((channels, bins_up), BF16),
            jax.ShapeDtypeStruct((bins_up, width), F32),
        ),
        [((bins_up, channels), F32)],
        4, macs // 4, first_block_kernel, second_block_kernel, first_block_bias[None],
        second_block_bias[None], head_weight, head_bias[None],
    )

    def strips(main, right, left):
        strip = rows(MARGIN + 2 * -(-MARGIN // per))
        down, up = call(strips_kernel, "strips", (strip, strip), [], 4, 1, main, right, left)
        return shifted(down, "col", 1), shifted(up, "col", -1)

    main, first, second = call(
        prepare_kernel, "prepare", (rows(size), packs, packs), [], 8, 1, pair_features
    )
    right, left = shifted(first, "row", -1), shifted(second, "row", 1)
    top, bottom = strips(main, right, left)
    kept_one, kept_two, hidden_inner, slope_one_inner, slope_two_inner, *sent_inner = call(
        forward_inner_kernel,
        "forward_inner",
        (
            sides(2 * d1), sides(d2), rows(inner), rows(size - 2 * d1, 2 * width, F32),
            rows(inner, width, F32), pieces(inner + 1), pieces(inner + 1),
        ),
        [
            ((size,) + ring, BF16), ((size - 2 * d1,) + ring, BF16),
            ((size + 2 * d1,) + ring, F32),
        ],
        18, 8 * macs, main, right, left, target, w1, b1, w2, b2,
    )
    got_inner = [lax.ppermute(sent_inner[k], ("row", "col"), mirror_pairs(k)) for k in range(2)]
    hidden_edge, slope_one_edge, slope_two_edge, *sent_edge = call(
        forward_edge_kernel,
        "forward_edge",
        (
            rows(2 * MARGIN), sides(MARGIN), rows(2 * MARGIN, width, F32),
            pieces(2 * MARGIN), pieces(2 * MARGIN),
        ),
        edge_rings,
        16, 4 * macs, top, bottom, kept_one, kept_two, w1, b1, w2, b2,
    )
    got_edge = [lax.ppermute(sent_edge[k], ("row", "col"), mirror_pairs(k)) for k in range(2)]

    delta, first, second = call(
        head_kernel,
        "head",
        (rows(size), packs, packs),
        [
            ((width * channels // 2, width), F32), ((size * channels, width), F32),
            ((size, width), jnp.int32),
        ],
        12, 4 * macs, *got_inner, *got_edge, hidden_inner, hidden_edge,
        slope_two_inner, slope_two_edge, target, weight, weight_t, bias,
    )
    right, left = shifted(first, "row", -1), shifted(second, "row", 1)
    top, bottom = strips(delta, right, left)
    w1, w2 = back_1, back_2
    kept_two, kept_one, inner_rows = call(
        backward_inner_kernel,
        "backward_inner",
        (sides(2 * d2), sides(d1), rows(inner, width, F32)),
        [
            ((size,) + ring, BF16), ((size - 2 * d2,) + ring, BF16),
            ((size + 2 * d2,) + ring, F32),
        ],
        18, 8 * macs, delta, right, left, slope_one_inner, w2, w1,
    )
    out = call(
        backward_edge_kernel,
        "backward_edge",
        jax.ShapeDtypeStruct((channels * size, width), F32),
        edge_rings,
        16, 4 * macs, top, bottom, kept_two, kept_one, inner_rows,
        slope_one_inner, slope_one_edge, w2, w1,
    )
    return out.reshape(channels, size, width)


def solution(mesh):
    in_specs = (P(None, "col", "row"), P(), P(), P(), P(), P(), P(), P("col", "row"))
    out_specs = P(None, "col", "row")
    return jax.shard_map(local, mesh=mesh, in_specs=in_specs, out_specs=out_specs, check_vma=False)
```

```python
import jax
import jax.numpy as jnp
from jax import lax
from jax.experimental import pallas as pl
from jax.experimental.pallas import tpu as pltpu
from jax.sharding import PartitionSpec as P

DILATION_FIRST = 4
DILATION_SECOND = 8
MARGIN = DILATION_FIRST + DILATION_SECOND
SLOT = 16
F32 = jnp.float32
BF16 = jnp.bfloat16
VMEM = pl.BlockSpec(memory_space=pltpu.VMEM)


def params(megabytes):
    return pltpu.CompilerParams(vmem_limit_bytes=megabytes << 20)


def lanes_of(shape):
    return lax.broadcasted_iota(jnp.int32, shape, len(shape) - 1)


def pack_edges(rows, first_ref, second_ref, block):
    count = len(rows)
    width = rows[0].shape[-1]
    slot = lanes_of(rows[0].shape) // SLOT
    first = second = None
    for i, row in enumerate(rows):
        turned = pltpu.roll(row, SLOT * i, 1) if i else row
        first = turned if first is None else jnp.where(slot == i, turned, first)
        second = turned if second is None else jnp.where(slot == (i - 1) % count, turned, second)
    first_ref[block] = first.astype(BF16)
    second_ref[block] = second.astype(BF16)


def ring_row(main, right, left, i):
    width = main.shape[-1]
    lane = lanes_of(main.shape)
    both = jnp.where(lane // SLOT == i, right.astype(F32), left.astype(F32))
    if i:
        both = pltpu.roll(both, width - SLOT * i, 1)
    edge = jnp.where((lane < MARGIN) | (lane >= width - MARGIN), both, 0.0)
    return jnp.concatenate([main, edge.astype(BF16)], axis=1)


def strip_ring(strip_ref, slots, ring_ref):
    per = ring_ref.shape[-1] // 2 // SLOT
    near = -(-MARGIN // per)
    for e in range(MARGIN):
        block, slot = divmod(e + slots, per)
        right, left = strip_ref[MARGIN + block], strip_ref[MARGIN + near + block]
        ring_ref[e] = ring_row(strip_ref[e], right, left, slot)


def main_ring(main_ref, right_ref, left_ref, ring_ref):
    per = main_ref.shape[-1] // SLOT

    @pl.loop(0, main_ref.shape[0] // per)
    def _(block):
        right = right_ref[block]
        left = left_ref[block]
        for slot in range(per):
            row = block * per + slot
            ring_ref[row] = ring_row(main_ref[row], right, left, slot)


def taps(row, spacing, width):
    wide = row.astype(F32)
    full = row.shape[-1]
    back = pltpu.roll(wide, spacing, 1)[:, :width]
    ahead = pltpu.roll(wide, full - spacing, 1)[:, :width]
    return jnp.concatenate([back.astype(BF16), row[:, :width], ahead.astype(BF16)], axis=0)


def wide_unit(source_ref, spacing):
    def unit(e):
        row = source_ref[e]
        return taps(row, spacing, row.shape[-1]), row.astype(F32)

    return unit


def narrow_unit(source_ref, spacing):
    width = source_ref.shape[-1] // 2

    def unit(e):
        rows = [source_ref[2 * e + k] for k in range(2)]
        both = jnp.concatenate([taps(row, spacing, width) for row in rows], axis=1)
        return both, jnp.concatenate([row[:, :width] for row in rows], axis=1).astype(F32)

    return unit


def inner_conv(unit, count, weights, reach, sums_ref, finish, unroll):
    channels = weights.shape[0] // 3

    def step(e, kind):
        seen, own = unit(e)
        z = jnp.dot(weights, seen, preferred_element_type=F32)
        middle, behind = z[channels : 2 * channels] + own, z[2 * channels :]
        if kind == 0:
            sums_ref[e] = behind
            sums_ref[e + reach] = middle
        else:
            total = sums_ref[e] + behind
            if kind == 1:
                sums_ref[e] = total
            else:
                finish(e - 2 * reach, total)
            sums_ref[e + reach] += middle
        sums_ref[e + 2 * reach] = z[:channels]

    for kind, begin, end in ((0, 0, reach), (1, reach, 2 * reach), (2, 2 * reach, count)):
        many = max(k for k in range(1, unroll + 1) if (end - begin) % k == 0)

        @pl.loop(begin, end, step=many)
        def _(e):
            for k in range(many):
                step(e + k, kind)


def keep_sums(sums_ref, count, reach, kept_ref):
    for k in range(2 * reach):
        kept_ref[0, k] = sums_ref[k]
        kept_ref[1, k] = sums_ref[count + k]


def edge_conv(unit, count, weights, reach, below, kept_ref, parts_ref, finish):
    channels = weights.shape[0] // 3
    for k in range(count):
        seen, own = unit(k)
        if below:
            taken = [t for t in range(3) if k + (2 - t) * reach < count]
        else:
            taken = [t for t in range(3) if k - t * reach >= 0]
        z = jnp.dot(
            weights[channels * taken[0] : channels * (taken[-1] + 1)],
            seen,
            preferred_element_type=F32,
        )
        for i, t in enumerate(taken):
            part = z[channels * i : channels * (i + 1)]
            parts_ref[k, t] = part + own if t == 1 else part
    for i in range(count):
        if below:
            total = parts_ref[i, 2]
            others = [(i - (2 - t) * reach, t) for t in range(2)]
            kept = i
        else:
            total = parts_ref[i, 0]
            others = [(i + t * reach, t) for t in (1, 2)]
            kept = i - count + 2 * reach
        for k, t in others:
            if 0 <= k < count:
                total = total + parts_ref[k, t]
        if 0 <= kept < 2 * reach:
            total = total + kept_ref[int(below), kept]
        finish(i, total)


def activated(pre):
    decay = jnp.exp(jnp.minimum(pre, 0.0))
    up = pre > 0
    return jnp.where(up, pre, decay - 1.0), jnp.where(up, 1.0, decay)


def lanes_inside(width):
    lane = lanes_of((1, 2 * width))
    q = jnp.where(lane < width + width // 2, lane, lane - 2 * width) + lax.axis_index("row") * width
    return jnp.where((q >= 0) & (q < lax.axis_size("row") * width), 1.0, 0.0)


def put_piece(send_refs, mine, p, hidden):
    channels, width = hidden.shape
    lo, hi = hidden[: channels // 2], hidden[channels // 2 :]
    low = lanes_of(lo.shape) < width // 2
    first = jnp.where(low, lo, pltpu.roll(hi, width // 2, 1)).astype(BF16)
    second = jnp.where(low, pltpu.roll(lo, width // 2, 1), hi).astype(BF16)
    swap = mine == 1
    send_refs[0][p] = jnp.where(swap, second, first)
    send_refs[1][p] = jnp.where(swap, first, second)


def prepare_kernel(x_ref, xt_ref, first_ref, second_ref):
    channels, size, width = x_ref.shape
    per = width // SLOT

    @pl.loop(0, size // per)
    def _(block):
        chunk = x_ref[:, pl.ds(block * per, per), :].astype(F32)
        turned = jnp.swapaxes(chunk, 0, 1)
        xt_ref[pl.ds(block * per, per)] = turned.astype(BF16)
        pack_edges([turned[i] for i in range(per)], first_ref, second_ref, block)


def weights_kernel(
    k1_ref, k2_ref, b1_ref, b2_ref, head_ref, head_bias_ref,
    ahead_1_ref, ahead_2_ref, back_1_ref, back_2_ref,
    column_1_ref, column_2_ref, head_up_ref, head_t_ref, head_column_ref,
    scratch_ref,
):
    for kernel_ref, ahead_ref, back_ref in (
        (k1_ref, ahead_1_ref, back_1_ref), (k2_ref, ahead_2_ref, back_2_ref)
    ):
        taps = [[kernel_ref[t, s].astype(F32) for s in range(3)] for t in range(3)]
        ahead = [jnp.concatenate(taps[t], axis=1) for t in range(3)]
        ahead_ref[...] = jnp.concatenate(ahead, axis=0).astype(BF16)
        back = [
            jnp.concatenate([taps[2 - t][2 - s].T for s in range(3)], axis=1) for t in range(3)
        ]
        back_ref[...] = jnp.concatenate(back, axis=0).astype(BF16)

    def column(row_ref):
        row = row_ref[...]
        return jnp.broadcast_to(row, (column_1_ref.shape[1], row.shape[1])).T

    column_1_ref[...] = column(b1_ref)
    column_2_ref[...] = column(b2_ref)
    bins = head_ref.shape[0]
    head_column_ref[...] = jnp.full(head_column_ref.shape, -jnp.inf, F32)
    head_column_ref[:bins] = column(head_bias_ref)
    scratch_ref[...] = jnp.zeros(scratch_ref.shape, F32)
    scratch_ref[:bins] = head_ref[...].astype(F32)
    head_up_ref[...] = scratch_ref[...].astype(BF16)
    head_t_ref[...] = scratch_ref[...].T.astype(BF16)


def strips_kernel(main_ref, right_ref, left_ref, down_ref, up_ref):
    size = main_ref.shape[0]
    blocks = right_ref.shape[0]
    near = (down_ref.shape[0] - MARGIN) // 2
    for k in range(MARGIN):
        down_ref[k] = main_ref[size - MARGIN + k]
        up_ref[k] = main_ref[k]
    for k in range(near):
        down_ref[MARGIN + k] = right_ref[blocks - near + k]
        down_ref[MARGIN + near + k] = left_ref[blocks - near + k]
        up_ref[MARGIN + k] = right_ref[k]
        up_ref[MARGIN + near + k] = left_ref[k]


def forward_inner_kernel(
    main_ref, right_ref, left_ref, target_ref, w1_ref, b1_ref, w2_ref, b2_ref,
    kept_one_ref, kept_two_ref, hidden_ref, slope_one_ref, slope_two_ref, send_a_ref, send_b_ref,
    ring_ref, near_ref, sums_ref,
):
    size, channels, width = main_ref.shape
    d1, d2 = DILATION_FIRST, DILATION_SECOND
    main_ring(main_ref, right_ref, left_ref, ring_ref)
    lane_ok = lanes_inside(width)
    mine = lax.rem(lax.axis_index("col"), width // size)
    b1 = jnp.concatenate([b1_ref[...]] * 2, axis=1)
    b2 = jnp.concatenate([b2_ref[...]] * 2, axis=1)

    def finish_one(i, total):
        hidden, slope = activated(total + b1)
        near_ref[i] = (hidden * lane_ok).astype(BF16)
        slope_one_ref[i] = slope * lane_ok

    inner_conv(wide_unit(ring_ref, d1), size, w1_ref[...], d1, sums_ref, finish_one, 8)
    keep_sums(sums_ref, size, d1, kept_one_ref)

    def finish_two(i, total):
        hidden, slope = activated(total + b2)
        for k in range(2):
            own = hidden[:, k * width : (k + 1) * width]
            hidden_ref[2 * i + k] = own.astype(BF16)
            slope_two_ref[2 * i + k] = slope[:, k * width : (k + 1) * width]
            put_piece((send_a_ref, send_b_ref), mine, 2 * i + k, own)

    count = near_ref.shape[0] // 2
    inner_conv(narrow_unit(near_ref, d2), count, w2_ref[...], d2 // 2, sums_ref, finish_two, 10)
    keep_sums(sums_ref, count, d2 // 2, kept_two_ref)
    put_piece((send_a_ref, send_b_ref), mine, size - 2 * MARGIN, target_ref[...].astype(F32))


def forward_edge_kernel(
    top_ref, bottom_ref, kept_one_ref, kept_two_ref, w1_ref, b1_ref, w2_ref, b2_ref,
    hidden_ref, slope_one_ref, slope_two_ref, send_a_ref, send_b_ref,
    ring_ref, near_ref, parts_ref,
):
    width = hidden_ref.shape[-1]
    size = width // 2
    d1, d2 = DILATION_FIRST, DILATION_SECOND
    lane_ok = lanes_inside(width)
    mine = lax.rem(lax.axis_index("col"), width // size)
    b1 = jnp.concatenate([b1_ref[...]] * 2, axis=1)
    b2 = jnp.concatenate([b2_ref[...]] * 2, axis=1)
    w1 = w1_ref[...]
    w2 = w2_ref[...]
    for below, strip_ref in enumerate((top_ref, bottom_ref)):
        ring, near = ring_ref.at[below], near_ref.at[below]
        parts = parts_ref.at[below]
        strip_ring(strip_ref, 0 if below else -MARGIN % (width // SLOT), ring)

        def finish_one(i, total):
            hidden, slope = activated(total + b1)
            p = (size - d1 if below else d1 - MARGIN) + i + lax.axis_index("col") * size
            ok = lane_ok * jnp.where((p >= 0) & (p < lax.axis_size("col") * size), 1.0, 0.0)
            near[i] = (hidden * ok).astype(BF16)
            slope_one_ref[below, i] = slope * ok

        edge_conv(
            wide_unit(ring, d1), MARGIN, w1, d1, below, kept_one_ref, parts, finish_one
        )

        def finish_two(i, total):
            hidden, slope = activated(total + b2)
            for k in range(2):
                row = below * MARGIN + 2 * i + k
                own = hidden[:, k * width : (k + 1) * width]
                hidden_ref[row] = own.astype(BF16)
                slope_two_ref[row] = slope[:, k * width : (k + 1) * width]
                put_piece((send_a_ref, send_b_ref), mine, row, own)

        edge_conv(
            narrow_unit(near, d2), MARGIN // 2, w2, d2 // 2, below, kept_two_ref, parts, finish_two
        )


def head_kernel(
    inner_a_ref, inner_b_ref, edge_a_ref, edge_b_ref,
    hidden_inner_ref, hidden_edge_ref, slope_inner_ref, slope_edge_ref, target_ref,
    weight_ref, weight_t_ref, bias_ref,
    delta_ref, first_ref, second_ref,
    wide_ref, turned_ref, target_t_ref,
):
    size, channels, width = delta_ref.shape
    half = channels // 2
    group = width // size
    mine = lax.rem(lax.axis_index("col"), group)
    inner = size - 2 * MARGIN

    def widen(source_a_ref, source_b_ref, row, p):
        wide_ref[pl.ds((mine * size + p) * half, half), :] = source_a_ref[row].astype(F32)
        wide_ref[pl.ds(((1 - mine) * size + p) * half, half), :] = source_b_ref[row].astype(F32)

    for k in range(inner):
        widen(inner_a_ref, inner_b_ref, k, k + MARGIN)
    for k in range(MARGIN):
        widen(edge_a_ref, edge_b_ref, k, k)
        widen(edge_a_ref, edge_b_ref, MARGIN + k, MARGIN + inner + k)

    @pl.loop(0, half, step=8)
    def _(c):
        for k in range(8):
            page = wide_ref[pl.ds(c + k, width, stride=half), :]
            page = page.T
            turned_ref[pl.ds(c + k, size, stride=channels), :] = page[:size]
            turned_ref[pl.ds(c + k + half, size, stride=channels), :] = page[size:]

    label_a = inner_a_ref[inner].astype(F32)
    label_b = inner_b_ref[inner].astype(F32)
    label_0 = jnp.where(mine == 0, label_a, label_b)
    label_1 = jnp.where(mine == 0, label_b, label_a)
    page = jnp.concatenate(
        [label_0, pltpu.roll(label_0, size, 1), label_1, pltpu.roll(label_1, size, 1)], axis=0
    )
    target_t_ref[...] = page.T[:size].astype(jnp.int32)

    bins = weight_ref.shape[0]
    weight = weight_ref[...]
    weight_t = weight_t_ref[...]
    bias = jnp.concatenate([bias_ref[...]] * 2, axis=1)
    bin_id = lax.broadcasted_iota(jnp.int32, (bins, 2 * width), 0)
    per = width // SLOT

    def own(p, inner_ref, edge_ref):
        if p < MARGIN:
            return edge_ref[p]
        return inner_ref[p - MARGIN] if p < MARGIN + inner else edge_ref[p - inner]

    def pair(p):
        symmetric = jnp.concatenate(
            [
                (
                    own(p + k, hidden_inner_ref, hidden_edge_ref).astype(F32)
                    + turned_ref[pl.ds((p + k) * channels, channels), :]
                ).astype(BF16)
                for k in range(2)
            ],
            axis=1,
        )
        logits = jnp.dot(weight, symmetric, preferred_element_type=F32) + bias
        top = jnp.max(logits, axis=0, keepdims=True)
        raised = jnp.exp(logits - top)
        probability = raised / jnp.sum(raised, axis=0, keepdims=True)
        labels = [
            jnp.concatenate([ref[pl.ds(p + k, 1), :] for k in range(2)], axis=1)
            for ref in (target_ref, target_t_ref)
        ]
        grads = [
            (probability - jnp.where(bin_id == label, 1.0, 0.0)).astype(BF16).astype(F32)
            for label in labels
        ]
        bins_sum = (grads[0] + grads[1]).astype(BF16)
        grad_two = jnp.dot(weight_t, bins_sum, preferred_element_type=F32)
        return [
            (
                grad_two[:, k * width : (k + 1) * width]
                * own(p + k, slope_inner_ref, slope_edge_ref)
            ).astype(BF16)
            for k in range(2)
        ]

    for block in range(size // per):
        deltas = []
        for k in range(0, per, 2):
            deltas += pair(block * per + k)
        for k in range(per):
            delta_ref[block * per + k] = deltas[k]
        pack_edges([d.astype(F32) for d in deltas], first_ref, second_ref, block)


def backward_inner_kernel(
    main_ref, right_ref, left_ref, slope_one_ref, w2_ref, w1_ref,
    kept_two_ref, kept_one_ref, rows_ref,
    ring_ref, near_ref, sums_ref,
):
    size, channels, width = main_ref.shape
    d1, d2 = DILATION_FIRST, DILATION_SECOND
    main_ring(main_ref, right_ref, left_ref, ring_ref)

    def finish_one(i, total):
        near_ref[i] = (total * slope_one_ref[i + d2 - d1]).astype(BF16)

    inner_conv(wide_unit(ring_ref, d2), size, w2_ref[...], d2, sums_ref, finish_one, 8)
    keep_sums(sums_ref, size, d2, kept_two_ref)

    def finish_two(i, total):
        for k in range(2):
            rows_ref[2 * i + k] = total[:, k * width : (k + 1) * width]

    count = near_ref.shape[0] // 2
    inner_conv(narrow_unit(near_ref, d1), count, w1_ref[...], d1 // 2, sums_ref, finish_two, 10)
    keep_sums(sums_ref, count, d1 // 2, kept_one_ref)


def backward_edge_kernel(
    top_ref, bottom_ref, kept_two_ref, kept_one_ref, rows_ref, slope_inner_ref, slope_edge_ref,
    w2_ref, w1_ref,
    out_ref,
    ring_ref, near_ref, parts_ref,
):
    inner, channels, width = rows_ref.shape
    size = inner + 2 * MARGIN
    d1, d2 = DILATION_FIRST, DILATION_SECOND
    w2 = w2_ref[...]
    w1 = w1_ref[...]

    def put(p, row):
        out_ref[pl.ds(p, channels, stride=size), :] = row

    for k in range(inner):
        put(k + MARGIN, rows_ref[k])
    for below, strip_ref in enumerate((top_ref, bottom_ref)):
        ring, near = ring_ref.at[below], near_ref.at[below]
        parts = parts_ref.at[below]
        strip_ring(strip_ref, 0 if below else -MARGIN % (width // SLOT), ring)

        def finish_one(i, total):
            p = (size - d2 if below else d2 - MARGIN) + i
            if d1 <= p < size - d1:
                slope = slope_inner_ref[p - d1]
            else:
                slope = slope_edge_ref[below, p - (size - d1 if below else d1 - MARGIN)]
            near[i] = (total * slope).astype(BF16)

        edge_conv(
            wide_unit(ring, d2), MARGIN, w2, d2, below, kept_two_ref, parts, finish_one
        )

        def finish_two(i, total):
            for k in range(2):
                p = below * (size - MARGIN) + 2 * i + k
                put(p, total[:, k * width : (k + 1) * width])

        edge_conv(
            narrow_unit(near, d1), MARGIN // 2, w1, d1 // 2, below, kept_one_ref, parts, finish_two
        )


def shifted(tensor, axis, step):
    count = lax.axis_size(axis)
    pairs = [(i, i + step) for i in range(count) if 0 <= i + step < count]
    return lax.ppermute(tensor, axis, pairs)


def routes(step):
    col_count, row_count = lax.axis_size("col"), lax.axis_size("row")
    group = col_count // row_count
    found = []
    for c in range(col_count):
        for r in range(row_count):
            owner = (c // group) * col_count + group * r + (c % group + step) % group
            relay = (r + row_count // 2) % row_count * col_count + c
            found.append((r * col_count + c, relay, owner))
    return found


def hop(tensor, step, begin, end):
    pairs = [(route[begin], route[end]) for route in routes(step)]
    return lax.ppermute(tensor, ("row", "col"), pairs)


def local(
    pair_features,
    first_block_kernel,
    first_block_bias,
    second_block_kernel,
    second_block_bias,
    head_weight,
    head_bias,
    target,
):
    channels, size, width = pair_features.shape
    d1, d2 = DILATION_FIRST, DILATION_SECOND
    per = width // SLOT
    def rows(count, lanes=width, kind=BF16):
        return jax.ShapeDtypeStruct((count, channels, lanes), kind)

    def sides(count, lanes=2 * width):
        return jax.ShapeDtypeStruct((2, count, channels, lanes), F32)

    def pieces(count):
        return jax.ShapeDtypeStruct((count, channels // 2, width), BF16)

    def call(kernel, name, outs, scratch, megabytes, flops, *operands):
        return pl.pallas_call(
            kernel,
            out_shape=outs,
            in_specs=[VMEM] * len(operands),
            out_specs=jax.tree.map(lambda _: VMEM, outs),
            scratch_shapes=[pltpu.VMEM(shape, kind) for shape, kind in scratch],
            compiler_params=params(megabytes),
            cost_estimate=pl.CostEstimate(flops=flops, bytes_accessed=8 << 20, transcendentals=0),
            name=name,
        )(*operands)

    inner = size - 2 * MARGIN
    ring = (channels, 2 * width)
    parts = ((2, MARGIN, 3) + ring, F32)
    edge_rings = [((2, MARGIN) + ring, BF16), ((2, MARGIN) + ring, BF16), parts]
    macs = 9 * channels * channels * size * width

    packs = rows(size // per)
    square = jax.ShapeDtypeStruct((3 * channels, 3 * channels), BF16)
    def strips(main, right, left):
        strip = rows(MARGIN + 2 * -(-MARGIN // per))
        down, up = call(strips_kernel, "strips", (strip, strip), [], 4, 1, main, right, left)
        return down, up

    main, first, second = call(
        prepare_kernel, "prepare", (rows(size), packs, packs), [], 8, 1, pair_features
    )
    right, left = shifted(first, "row", -1), shifted(second, "row", 1)
    down, up = strips(main, right, left)
    bins = head_weight.shape[0]
    bins_up = -(-bins // 16) * 16
    column = jax.ShapeDtypeStruct((channels, width), F32)
    tensors, down, up = lax.optimization_barrier(
        (
            (
                first_block_kernel, second_block_kernel, first_block_bias[None],
                second_block_bias[None], head_weight, head_bias[None],
            ),
            down, up,
        )
    )
    w1, w2, back_1, back_2, b1, b2, weight, weight_t, bias = call(
        weights_kernel,
        "weights",
        (square,) * 4 + (
            column, column, jax.ShapeDtypeStruct((bins_up, channels), BF16),
            jax.ShapeDtypeStruct((channels, bins_up), BF16),
            jax.ShapeDtypeStruct((bins_up, width), F32),
        ),
        [((bins_up, channels), F32)],
        4, macs // 4, *tensors,
    )
    top, bottom = shifted(down, "col", 1), shifted(up, "col", -1)
    kept_one, kept_two, hidden_inner, slope_one_inner, slope_two_inner, *sent_inner = call(
        forward_inner_kernel,
        "forward_inner",
        (
            sides(2 * d1), sides(d2), rows(inner), rows(size - 2 * d1, 2 * width, F32),
            rows(inner, width, F32), pieces(inner + 1), pieces(inner + 1),
        ),
        [
            ((size,) + ring, BF16), ((size - 2 * d1,) + ring, BF16),
            ((size + 2 * d1,) + ring, F32),
        ],
        18, 8 * macs, main, right, left, target, w1, b1, w2, b2,
    )
    relayed = hop(sent_inner[0], 0, 0, 1)
    got_inner_b = hop(sent_inner[1], 1, 0, 2)
    hidden_edge, slope_one_edge, slope_two_edge, *sent_edge = call(
        forward_edge_kernel,
        "forward_edge",
        (
            rows(2 * MARGIN), sides(MARGIN), rows(2 * MARGIN, width, F32),
            pieces(2 * MARGIN), pieces(2 * MARGIN),
        ),
        edge_rings,
        16, 4 * macs, top, bottom, kept_one, kept_two, w1, b1, w2, b2,
    )
    relayed, *sent_edge = lax.optimization_barrier((relayed, *sent_edge))
    got_inner = [hop(relayed, 0, 1, 2), got_inner_b]
    got_edge = [hop(sent_edge[k], k, 0, 2) for k in range(2)]

    delta, first, second = call(
        head_kernel,
        "head",
        (rows(size), packs, packs),
        [
            ((width * channels // 2, width), F32), ((size * channels, width), F32),
            ((size, width), jnp.int32),
        ],
        12, 4 * macs, *got_inner, *got_edge, hidden_inner, hidden_edge,
        slope_two_inner, slope_two_edge, target, weight, weight_t, bias,
    )
    right, left = shifted(first, "row", -1), shifted(second, "row", 1)
    down, up = strips(delta, right, left)
    top, bottom = shifted(down, "col", 1), shifted(up, "col", -1)
    w1, w2 = back_1, back_2
    kept_two, kept_one, inner_rows = call(
        backward_inner_kernel,
        "backward_inner",
        (sides(2 * d2), sides(d1), rows(inner, width, F32)),
        [
            ((size,) + ring, BF16), ((size - 2 * d2,) + ring, BF16),
            ((size + 2 * d2,) + ring, F32),
        ],
        18, 8 * macs, delta, right, left, slope_one_inner, w2, w1,
    )
    out = call(
        backward_edge_kernel,
        "backward_edge",
        jax.ShapeDtypeStruct((channels * size, width), F32),
        edge_rings,
        16, 4 * macs, top, bottom, kept_two, kept_one, inner_rows,
        slope_one_inner, slope_one_edge, w2, w1,
    )
    return out.reshape(channels, size, width)


def solution(mesh):
    in_specs = (P(None, "col", "row"), P(), P(), P(), P(), P(), P(), P("col", "row"))
    out_specs = P(None, "col", "row")
    return jax.shard_map(local, mesh=mesh, in_specs=in_specs, out_specs=out_specs, check_vma=False)
```
